32 devices in a mesh: rep: 4 (over y, core), shard: 8 (over z, x).
Axes of the slice: x: 2, y: 2, z: 4, core: 2. Of those that a mesh axis runs over, the one named last changes fastest.
Arguments:
- hidden_in: bfloat16 [8192, 1024], P(('rep', 'shard')), may hold values from -6 to 6
- cotangent: bfloat16 [8192, 1024], P(('rep', 'shard')), may hold values from -6 to 6
- ln1_gain: bfloat16 [1024], P('shard'), may hold values from 0.5 to 1.5
- ln1_bias: bfloat16 [1024], P('shard'), may hold values from -3 to 3
- w_qkv: bfloat16 [1024, 3072], P('shard'), may hold values from -16 to 16
- qv_bias: bfloat16 [2048], P('shard'), may hold values from -3 to 3
- w_dense: bfloat16 [1024, 1024], P('shard'), may hold values from -0.75 to 0.75
- dense_bias: bfloat16 [1024], P('shard'), may hold values from -3 to 3
- ln2_gain: bfloat16 [1024], P('shard'), may hold values from 0.5 to 1.5
- ln2_bias: bfloat16 [1024], P('shard'), may hold values from -3 to 3
- w_up: bfloat16 [1024, 4096], P('shard'), may hold values from -0.1875 to 0.1875
- up_bias: bfloat16 [4096], P('shard'), may hold values from -3 to 3
- w_down: bfloat16 [4096, 1024], P('shard'), may hold values from -0.09375 to 0.09375
- down_bias: bfloat16 [1024], P('shard'), may hold values from -3 to 3
Outputs:
- output: bfloat16 [8192, 1024], P(('rep', 'shard'))
- input_grad: float32 [8192, 1024], P(('rep', 'shard'))
- grad_ln1_gain: float32 [1024], P('shard')
- grad_ln1_bias: float32 [1024], P('shard')
- grad_qkv: float32 [1024, 3072], P('shard')
- grad_qv_bias: float32 [2048], P('shard')
- grad_dense: float32 [1024, 1024], P('shard')
- grad_dense_bias: float32 [1024], P('shard')
- grad_ln2_gain: float32 [1024], P('shard')
- grad_ln2_bias: float32 [1024], P('shard')
- grad_up: float32 [1024, 4096], P('shard')
- grad_up_bias: float32 [4096], P('shard')
- grad_down: float32 [4096, 1024], P('shard')
- grad_down_bias: float32 [1024], P('shard')
The draws below stay inside these ranges and needn't reach their ends.
All inputs are finite; a program needn't handle non-finite values.
Results may differ from the reference program's by a relative error of at most 0.0092.
Values may be sent and summed in bfloat16 or wider, within the bound.
No kernel may reach another device: no remote copies, remote signals or barrier semaphores. Data moves between devices by JAX's collectives and lax.ppermute only.
A program may use at most 192 MiB of HBM per device.

```python
import math
import jax
import jax.numpy as jnp
from jax import lax

D = 1024
FF = 4096
H = 16
L = 256
TOKENS = 8192


def draw_w_qkv(key, part):
    base_draw = jnp.clip(jax.random.normal(key, (D, 3 * D), jnp.float32), -6.0, 6.0) * D ** (-0.5)
    return base_draw.astype(jnp.bfloat16)


def block_scale(key, shape, cuts, smallest, top_value):
    factor_of, own = 1.0, jax.random.fold_in(key, 6)
    for dim, shards_of in cuts:
        draws = jnp.exp(jax.random.uniform(jax.random.fold_in(own, dim), (shards_of,), jnp.float32, smallest / len(cuts), top_value / len(cuts)))
        factor_of = factor_of * jnp.repeat(draws, shape[dim] // shards_of).reshape([-1 if axis == dim else 1 for axis in range(len(shape))])
    return factor_of


def noise(stream_key, dims, scale, reach, split=(), kind=jnp.bfloat16):
    result = jax.random.normal(stream_key, dims, jnp.float32) * scale
    if len(split) > 0:
        result = block_scale(stream_key, dims, split, -0.22, 0.18) * result
    return jnp.clip(result, min=-reach, max=reach).astype(kind)


def setup_inputs(seed: int = 0) -> dict:
    key_of = jax.random.split(jax.random.key(seed), 15)
    return {
        "hidden_in": noise(key_of[0], (TOKENS, D), 1.0, 6.0, ((0, 32),)),
        "cotangent": noise(key_of[1], (TOKENS, D), 1.0, 6.0, ((0, 32),)),
        "ln1_gain": jnp.clip(1.0 + 0.1 * jax.random.normal(key_of[2], (D,), jnp.float32), 0.5, 1.5).astype(jnp.bfloat16),
        "ln1_bias": noise(key_of[3], (D,), 0.5, 3.0, ((0, 8),)),
        "w_qkv": draw_w_qkv(jax.random.fold_in(key_of[14], 71), 0),
        "qv_bias": noise(key_of[5], (2 * D,), 0.5, 3.0, ((0, 8),)),
        "w_dense": noise(key_of[6], (D, D), (D // 16) ** -0.5, 0.75, ((0, 8),)),
        "dense_bias": noise(key_of[7], (D,), 0.5, 3.0, ((0, 8),)),
        "ln2_gain": jnp.clip(1.0 + 0.1 * jax.random.normal(key_of[8], (D,), jnp.float32), 0.5, 1.5).astype(jnp.bfloat16),
        "ln2_bias": noise(key_of[9], (D,), 0.5, 3.0, ((0, 8),)),
        "w_up": noise(key_of[10], (D, FF), D ** -0.5, 0.1875, ((0, 8),)),
        "up_bias": noise(key_of[11], (FF,), 0.5, 3.0, ((0, 8),)),
        "w_down": noise(key_of[12], (FF, D), FF ** -0.5, 0.09375, ((0, 8),)),
        "down_bias": noise(key_of[13], (D,), 0.5, 3.0, ((0, 8),)),
    }


gelu_coef = math.sqrt(2.0 / math.pi)

def head_slopes(head_count):
    return 2.0 ** (-8.0 * (jnp.arange(head_count, dtype=jnp.float32) + 1.0) / head_count)

def rounded(values_in):
    return lax.optimization_barrier(values_in.astype(jnp.bfloat16)).astype(jnp.float32)

def layer_norm(values_in):
    centre = values_in - lax.optimization_barrier(jnp.mean(values_in, axis=-1, keepdims=True))
    inv_std = lax.rsqrt(lax.optimization_barrier(jnp.mean(centre * centre, axis=-1, keepdims=True)) + 1e-05)
    return (centre * inv_std, inv_std)

def norm_back(grad_normed, normed, inv_std):
    return inv_std * (grad_normed - lax.optimization_barrier(jnp.mean(grad_normed, axis=-1, keepdims=True)) - normed * lax.optimization_barrier(jnp.mean(grad_normed * normed, axis=-1, keepdims=True)))

def gelu_value(pre_gelu):
    return 0.5 * pre_gelu * (1.0 + jnp.tanh(gelu_coef * (pre_gelu + 0.044715 * pre_gelu ** 3)))

def gelu_slope(pre_gelu):
    tanh_part = jnp.tanh(gelu_coef * (pre_gelu + 0.044715 * pre_gelu ** 3))
    return 0.5 * (1.0 + tanh_part) + 0.5 * pre_gelu * (1.0 - tanh_part * tanh_part) * gelu_coef * (1.0 + 3.0 * 0.044715 * pre_gelu * pre_gelu)

def split_heads(matrix, head_count):
    return matrix.reshape(matrix.shape[0], head_count, matrix.shape[1] // head_count)

def masked_scores(query_heads, key_heads, row_start, slopes):
    block_rows = query_heads.shape[0]
    key_count = key_heads.shape[0]
    scale_factor = query_heads.shape[2] ** (-0.5)
    raw_scores = jnp.einsum('qhd,khd->hqk', query_heads.astype(jnp.float32), key_heads.astype(jnp.float32))
    query_pos = row_start + jnp.arange(block_rows)
    key_pos = jnp.arange(key_count)
    distance = (key_pos[None, :] - query_pos[:, None]).astype(jnp.float32)
    scores = raw_scores * scale_factor + slopes[:, None, None] * distance[None, :, :]
    return jnp.where((key_pos[None, :] <= query_pos[:, None])[None, :, :], scores, -1e+30)

def attend(queries, key_rows, value_rows, slopes):
    head_count = slopes.shape[0]
    query_heads = split_heads(queries, head_count)
    key_heads = split_heads(key_rows, head_count)
    value_heads = split_heads(value_rows, head_count)
    length = queries.shape[0]
    block_rows = min(length, 512)
    contexts = []
    totals = []
    for row_start in range(0, length, block_rows):
        scores = masked_scores(query_heads[row_start:row_start + block_rows], key_heads, row_start, slopes)
        maximum = lax.optimization_barrier(jnp.max(scores, axis=-1, keepdims=True))
        log_total = maximum + jnp.log(lax.optimization_barrier(jnp.sum(jnp.exp(scores - maximum), axis=-1, keepdims=True)))
        attn_probs = rounded(jnp.exp(scores - log_total))
        context = jnp.einsum('hqk,khd->qhd', attn_probs, value_heads.astype(jnp.float32))
        contexts.append(context.reshape(block_rows, -1).astype(jnp.bfloat16))
        totals.append(log_total)
    return (jnp.concatenate(contexts, axis=0), jnp.concatenate(totals, axis=1))

def attend_back(queries, key_rows, value_rows, log_totals, grad_context, slopes):
    head_count = slopes.shape[0]
    query_heads = split_heads(queries, head_count)
    key_heads = split_heads(key_rows, head_count)
    value_heads = split_heads(value_rows, head_count)
    length = queries.shape[0]
    block_rows = min(length, 512)
    scale_factor = query_heads.shape[2] ** (-0.5)
    grad_keys = jnp.zeros(key_heads.shape, jnp.float32)
    grad_values = jnp.zeros(value_heads.shape, jnp.float32)
    query_parts = []
    for row_start in range(0, length, block_rows):
        query_block = query_heads[row_start:row_start + block_rows]
        scores = masked_scores(query_block, key_heads, row_start, slopes)
        probs_again = jnp.exp(scores - log_totals[:, row_start:row_start + block_rows])
        grad_block = grad_context[row_start:row_start + block_rows].reshape(block_rows, head_count, -1)
        grad_probs = jnp.einsum('qhd,khd->hqk', grad_block.astype(jnp.float32), value_heads.astype(jnp.float32))
        grad_scores = rounded(probs_again * (grad_probs - lax.optimization_barrier(jnp.sum(probs_again * grad_probs, axis=-1, keepdims=True))) * scale_factor)
        query_parts.append(jnp.einsum('hqk,khd->qhd', grad_scores, key_heads.astype(jnp.float32)).reshape(block_rows, -1))
        grad_keys = grad_keys + jnp.einsum('hqk,qhd->khd', grad_scores, query_block.astype(jnp.float32))
        grad_values = grad_values + jnp.einsum('hqk,qhd->khd', rounded(probs_again), grad_block.astype(jnp.float32))
    return (jnp.concatenate(query_parts, axis=0), grad_keys.reshape(length, -1), grad_values.reshape(length, -1))

def block_layer(hidden_rows, grad_rows, weights, slopes):
    ln1_gain, ln1_bias, w_qkv, qv_bias, w_dense, dense_bias, ln2_gain, ln2_bias, w_up, up_bias, w_down, down_bias = weights
    width = hidden_rows.shape[1]
    gain_one = ln1_gain.astype(jnp.float32)
    gain_two = ln2_gain.astype(jnp.float32)
    input_rows = hidden_rows.astype(jnp.float32)
    normed_one, inv_one = layer_norm(input_rows)
    normed_in = (normed_one * gain_one + ln1_bias.astype(jnp.float32)).astype(jnp.bfloat16)
    projected = jnp.dot(normed_in, w_qkv, preferred_element_type=jnp.float32)
    queries = (projected[:, :width] + qv_bias[:width].astype(jnp.float32)).astype(jnp.bfloat16)
    key_rows = projected[:, width:2 * width].astype(jnp.bfloat16)
    value_rows = (projected[:, 2 * width:] + qv_bias[width:].astype(jnp.float32)).astype(jnp.bfloat16)
    context, log_totals = attend(queries, key_rows, value_rows, slopes)
    residual = input_rows + jnp.dot(context, w_dense, preferred_element_type=jnp.float32) + dense_bias.astype(jnp.float32)
    normed_two, inv_two = layer_norm(residual)
    normed_mid = (normed_two * gain_two + ln2_bias.astype(jnp.float32)).astype(jnp.bfloat16)
    pre_gelu = jnp.dot(normed_mid, w_up, preferred_element_type=jnp.float32) + up_bias.astype(jnp.float32)
    activated = gelu_value(pre_gelu).astype(jnp.bfloat16)
    output = (residual + jnp.dot(activated, w_down, preferred_element_type=jnp.float32) + down_bias.astype(jnp.float32)).astype(jnp.bfloat16)
    grad_out = grad_rows.astype(jnp.float32)
    grad_down = jnp.dot(activated.T, grad_rows, preferred_element_type=jnp.float32)
    grad_down_bias = lax.optimization_barrier(jnp.sum(grad_out, axis=0))
    grad_pre = jnp.dot(grad_rows, w_down.T, preferred_element_type=jnp.float32) * gelu_slope(pre_gelu)
    grad_pre_b = grad_pre.astype(jnp.bfloat16)
    grad_up = jnp.dot(normed_mid.T, grad_pre_b, preferred_element_type=jnp.float32)
    grad_up_bias = lax.optimization_barrier(jnp.sum(grad_pre, axis=0))
    grad_mid = jnp.dot(grad_pre_b, w_up.T, preferred_element_type=jnp.float32)
    grad_ln2_gain = lax.optimization_barrier(jnp.sum(grad_mid * normed_two, axis=0))
    grad_ln2_bias = lax.optimization_barrier(jnp.sum(grad_mid, axis=0))
    grad_residual = grad_out + norm_back(grad_mid * gain_two, normed_two, inv_two)
    grad_res_b = grad_residual.astype(jnp.bfloat16)
    grad_dense = jnp.dot(context.T, grad_res_b, preferred_element_type=jnp.float32)
    grad_dense_bias = lax.optimization_barrier(jnp.sum(grad_residual, axis=0))
    grad_context = jnp.dot(grad_res_b, w_dense.T, preferred_element_type=jnp.float32).astype(jnp.bfloat16)
    grad_queries, grad_keys, grad_values = attend_back(queries, key_rows, value_rows, log_totals, grad_context, slopes)
    grad_qv_bias = jnp.concatenate([lax.optimization_barrier(jnp.sum(grad_queries, axis=0)), lax.optimization_barrier(jnp.sum(grad_values, axis=0))])
    grad_qkv_b = jnp.concatenate([grad_queries, grad_keys, grad_values], axis=1).astype(jnp.bfloat16)
    grad_qkv = jnp.dot(normed_in.T, grad_qkv_b, preferred_element_type=jnp.float32)
    grad_normed = jnp.dot(grad_qkv_b, w_qkv.T, preferred_element_type=jnp.float32)
    grad_ln1_gain = lax.optimization_barrier(jnp.sum(grad_normed * normed_one, axis=0))
    grad_ln1_bias = lax.optimization_barrier(jnp.sum(grad_normed, axis=0))
    input_grad = grad_residual + norm_back(grad_normed * gain_one, normed_one, inv_one)
    grads = (grad_ln1_gain, grad_ln1_bias, grad_qkv, grad_qv_bias, grad_dense, grad_dense_bias, grad_ln2_gain, grad_ln2_bias, grad_up, grad_up_bias, grad_down, grad_down_bias)
    return (output, input_grad, grads)

def reference(hidden_in, cotangent, ln1_gain, ln1_bias, w_qkv, qv_bias, w_dense, dense_bias, ln2_gain, ln2_bias, w_up, up_bias, w_down, down_bias):
    weights = (ln1_gain, ln1_bias, w_qkv, qv_bias, w_dense, dense_bias, ln2_gain, ln2_bias, w_up, up_bias, w_down, down_bias)
    slopes = head_slopes(H)
    seq_count = hidden_in.shape[0] // L
    hidden_seqs = hidden_in.reshape(seq_count, L, D)
    grad_seqs = cotangent.reshape(seq_count, L, D)
    initial = tuple((jnp.zeros(weight_arg.shape, jnp.float32) for weight_arg in weights))

    def one_seq(running, seq_pair):
        output, input_grad, grads = block_layer(seq_pair[0], seq_pair[1], weights, slopes)
        summed = tuple((left_sum + right_sum for left_sum, right_sum in zip(running, grads)))
        return (summed, (output, input_grad))
    totals, (outputs, input_grads) = lax.scan(one_seq, initial, (hidden_seqs, grad_seqs))
    return (outputs.reshape(-1, D), input_grads.reshape(-1, D), totals[0], totals[1], totals[2], totals[3], totals[4], totals[5], totals[6], totals[7], totals[8], totals[9], totals[10], totals[11])
```

```python
import functools
import math

import jax
import jax.numpy as jnp
from jax import lax
from jax.sharding import PartitionSpec as P

H = 16
BF = jnp.bfloat16
F32 = jnp.float32
AXES = ("rep", "shard")
gelu_coef = math.sqrt(2.0 / math.pi)


class Place:
    def __init__(self, reps, shards):
        self.reps, self.shards = reps, shards
        self.nx = max(n for n in (1, 2, 4, 8) if shards % n == 0 and n * n <= shards)
        self.nz = shards // self.nx
        rep, shard = lax.axis_index("rep"), lax.axis_index("shard")
        self.y, self.core = rep // 2, rep % 2
        self.z, self.x = shard // self.nx, shard % self.nx
        self.shard = shard

    def _send(self, value, move):
        pairs = []
        for rep in range(self.reps):
            for shard in range(self.shards):
                y, core, z, x = move(rep // 2, rep % 2, shard // self.nx, shard % self.nx)
                pairs.append((rep * self.shards + shard, (y * 2 + core) * self.shards + z * self.nx + x))
        return lax.ppermute(value, AXES, pairs)

    def to_core(self, value):
        return self._send(value, lambda y, core, z, x: (y, 1 - core, z, x))

    def to_y(self, value):
        return self._send(value, lambda y, core, z, x: (1 - y, core, z, x))

    def to_z(self, value, k):
        return self._send(value, lambda y, core, z, x: (y, core, (z + k) % self.nz, x))

    def to_x(self, value, k):
        return self._send(value, lambda y, core, z, x: (y, core, z, (x + k) % self.nx))

    def from_shard(self, kz, kx):
        z, x = lax.rem(self.z - kz + self.nz, self.nz), lax.rem(self.x - kx + self.nx, self.nx)
        return z * self.nx + x

    def gather_slots(self, block):
        slots = {}
        for kz in range(self.nz):
            held = block if kz == 0 else self.to_z(block, kz)
            for kx in range(self.nx):
                slots[kz, kx] = held if kx == 0 else self.to_x(held, kx)
        return slots

    def assemble(self, slots):
        first = slots[0, 0]
        whole = jnp.zeros((self.shards * first.shape[0],) + first.shape[1:], first.dtype)
        for (kz, kx), block in slots.items():
            start = self.from_shard(kz, kx) * first.shape[0]
            whole = lax.dynamic_update_slice(whole, block, (start,) + (0,) * (first.ndim - 1))
        return whole

    def sum_all(self, value):
        value = value + self.to_core(value)
        value = value + self.to_y(value)
        value = sum([self.to_x(value, k) for k in range(1, self.nx)], value)
        return sum([self.to_z(value, k) for k in range(1, self.nz)], value)

    def near_first(self):
        return sorted(range(self.nz), key=lambda k: -min(k, self.nz - k))

    def _owner_sum(self, chunk_of):
        terms = []
        for k in self.near_first():
            chunk = chunk_of(k)
            mine = lax.dynamic_index_in_dim(chunk, self.x, 0, keepdims=False)
            for kx in range(1, self.nx):
                other = lax.rem(self.x + kx, self.nx)
                away = lax.dynamic_index_in_dim(chunk, other, 0, keepdims=False).astype(BF)
                mine = mine + self.to_x(away, kx).astype(F32)
            terms.append(mine if k == 0 else self.to_z(mine.astype(BF), k).astype(F32))
        return functools.reduce(lambda a, b: a + b, terms)

    def scatter_xz(self, chunk_of):
        part = lax.optimization_barrier(self._owner_sum(chunk_of).astype(BF))
        return part.astype(F32) + self.to_y(part).astype(F32)

    def scatter_yxz(self, away_of, mine_of):
        def chunk_of(k):
            return mine_of(k) + self.to_y(away_of(k).astype(BF)).astype(F32)

        part = lax.optimization_barrier(self._owner_sum(chunk_of).astype(BF))
        return part, self.to_y(part)


def head_slopes(head_count):
    return 2.0 ** (-8.0 * (jnp.arange(head_count, dtype=F32) + 1.0) / head_count)


def layer_norm(values_in):
    centre = values_in - jnp.mean(values_in, axis=-1, keepdims=True)
    inv_std = lax.rsqrt(jnp.mean(centre * centre, axis=-1, keepdims=True) + 1e-05)
    return (centre * inv_std, inv_std)


def norm_back(grad_normed, normed, inv_std):
    return inv_std * (
        grad_normed
        - jnp.mean(grad_normed, axis=-1, keepdims=True)
        - normed * jnp.mean(grad_normed * normed, axis=-1, keepdims=True)
    )


def gelu_both(u):
    t = jnp.tanh(gelu_coef * (u + 0.044715 * u * u * u))
    value = 0.5 * u * (1.0 + t)
    slope = 0.5 * (1.0 + t) + 0.5 * u * (1.0 - t * t) * gelu_coef * (1.0 + 3.0 * 0.044715 * u * u)
    return value, slope


def dot(a, b):
    return jnp.dot(a, b, preferred_element_type=F32)


def dot_tn(a, b):
    return lax.dot_general(a, b, (((0,), (0,)), ((), ())), preferred_element_type=F32)


def dot_nt(a, b):
    return lax.dot_general(a, b, (((1,), (1,)), ((), ())), preferred_element_type=F32)


def pick(pair_first, pair_second, index):
    flip = index == 1
    return jnp.where(flip, pair_second, pair_first), jnp.where(flip, pair_first, pair_second)


def on_device(
    reps,
    shards,
    hidden_in,
    cotangent,
    ln1_gain,
    ln1_bias,
    w_qkv,
    qv_bias,
    w_dense,
    dense_bias,
    ln2_gain,
    ln2_bias,
    w_up,
    up_bias,
    w_down,
    down_bias,
):
    at = Place(reps, shards)
    core, y = at.core, at.y
    rows, width = hidden_in.shape
    rd = w_qkv.shape[0]
    ff = w_up.shape[1]
    quarter = ff // shards // 4
    half = width // 2
    heads = H // 2
    hd = width // H
    slopes = lax.dynamic_slice_in_dim(head_slopes(H), core * heads, heads)

    vectors = (ln1_gain, ln1_bias, qv_bias, dense_bias, ln2_gain, ln2_bias, up_bias, down_bias)
    packed = jnp.concatenate(vectors)[None, :]
    packed = at.assemble(at.gather_slots(packed))
    whole, start = [], 0
    for v in vectors:
        whole.append(packed[:, start : start + v.shape[0]].reshape(-1).astype(F32))
        start += v.shape[0]
    gain1, bias1, qv_b, dense_b, gain2, bias2, up_b, down_b = whole

    qkv_half = lax.dynamic_index_in_dim(w_qkv.reshape(rd, 3, 2, half), core, 2, keepdims=False)
    qkv_half = qkv_half.reshape(rd, 3 * half)
    dense_half = lax.dynamic_slice_in_dim(w_dense, core * half, half, 1)
    up_quarter = w_up.reshape(rd, shards, 2, 2, quarter)
    up_quarter = lax.dynamic_index_in_dim(up_quarter, core, 2, keepdims=False)
    up_quarter = lax.dynamic_index_in_dim(up_quarter, y, 2, keepdims=False).reshape(rd, shards * quarter)
    down_quarter = lax.dynamic_slice_in_dim(w_down, (core * 2 + y) * quarter, quarter, 0)

    input_rows = hidden_in.astype(F32)
    normed_one, inv_one = layer_norm(input_rows)
    normed_in = (normed_one * gain1 + bias1).astype(BF)
    normed_in = jnp.concatenate([normed_in, at.to_core(normed_in)])
    cot = jnp.concatenate([cotangent, at.to_core(cotangent)])

    wq = at.assemble(at.gather_slots(qkv_half))
    wd = at.assemble(at.gather_slots(dense_half))
    wd_other = at.to_core(wd)
    up_slots = at.gather_slots(up_quarter)
    wu = (at.assemble(up_slots), at.assemble({k: at.to_y(v) for k, v in up_slots.items()}))
    down_slots = at.gather_slots(down_quarter)
    wo = (at.assemble(down_slots), at.assemble({k: at.to_y(v) for k, v in down_slots.items()}))
    wd = jnp.concatenate(pick(wd, wd_other, core), axis=1)

    projected = dot(normed_in, wq)
    q_b = lax.dynamic_slice_in_dim(qv_b[:width], core * half, half)
    v_b = lax.dynamic_slice_in_dim(qv_b[width:], core * half, half)
    queries = (projected[:, :half] + q_b).astype(BF).reshape(2, rows, heads, hd)
    keys = projected[:, half : 2 * half].astype(BF).reshape(2, rows, heads, hd)
    values = (projected[:, 2 * half :] + v_b).astype(BF).reshape(2, rows, heads, hd)
    raw = jnp.einsum("bqhd,bkhd->bhqk", queries, keys, preferred_element_type=F32)
    pos = jnp.arange(rows)
    distance = (pos[None, :] - pos[:, None]).astype(F32)
    scores = raw * hd ** (-0.5) + slopes[None, :, None, None] * distance
    scores = jnp.where(pos[None, :] <= pos[:, None], scores, -1e30)
    maximum = jnp.max(scores, axis=-1, keepdims=True)
    log_total = maximum + jnp.log(jnp.sum(jnp.exp(scores - maximum), axis=-1, keepdims=True))
    probs = jnp.exp(scores - log_total)
    probs_b = probs.astype(BF)
    context = jnp.einsum("bhqk,bkhd->bqhd", probs_b, values, preferred_element_type=F32)
    context = context.astype(BF).reshape(2, rows, half)
    context = jnp.concatenate(pick(context[0], at.to_core(context[1]), core), axis=1)

    residual = input_rows + dot(context, wd) + dense_b
    normed_two, inv_two = layer_norm(residual)
    normed_mid = (normed_two * gain2 + bias2).astype(BF)
    normed_mid = jnp.concatenate([normed_mid, at.to_core(normed_mid)])

    up_b4 = lax.dynamic_index_in_dim(up_b.reshape(shards, 2, 2, quarter), core, 1, keepdims=False)
    up_bs = pick(up_b4[:, 0].reshape(-1), up_b4[:, 1].reshape(-1), y)
    acts, slope_of = [], []
    for w, b in zip(wu, up_bs):
        value, slope = gelu_both(dot(normed_mid, w) + b)
        acts.append(value.astype(BF))
        slope_of.append(slope)
    part = dot(acts[0], wo[0]) + dot(acts[1], wo[1])
    output = (residual + part[:rows] + at.to_core(part[rows:]) + down_b).astype(BF)

    nz, nx = at.nz, at.nx

    def owner_cols(matrix, k, per):
        z = lax.rem(at.z + k, nz)
        return lax.dynamic_slice_in_dim(matrix, z * nx * per, nx * per, 1)

    def down_terms(i):
        return lambda k: dot_tn(owner_cols(acts[i], k, quarter), cot).reshape(nx, quarter, width)

    down_own, down_other = at.scatter_yxz(down_terms(1), down_terms(0))
    grad_down_bias = jnp.sum(cotangent.astype(F32), axis=0)
    grad_pre = [dot_nt(cot, w) * s for w, s in zip(wo, slope_of)]
    grad_pre_b = [g.astype(BF) for g in grad_pre]
    grad_up_bias = [jnp.sum(g, axis=0) for g in grad_pre]
    both_pre = jnp.concatenate(grad_pre_b, axis=1)

    def up_terms(k):
        return dot_tn(owner_cols(normed_mid, k, rd), both_pre).reshape(nx, rd, 2 * shards * quarter)

    def up_terms_by_y(k):
        terms = up_terms(k).reshape(nx, rd, 2, shards * quarter)
        return jnp.concatenate(pick(terms[:, :, 0], terms[:, :, 1], y), axis=-1)

    up_total = at.scatter_xz(up_terms_by_y)
    gmid = dot_nt(grad_pre_b[0], wu[0]) + dot_nt(grad_pre_b[1], wu[1])
    grad_mid = gmid[:rows] + at.to_core(gmid[rows:])
    grad_ln2_gain = jnp.sum(grad_mid * normed_two, axis=0)
    grad_ln2_bias = jnp.sum(grad_mid, axis=0)
    grad_residual = cotangent.astype(F32) + norm_back(grad_mid * gain2, normed_two, inv_two)
    grad_res_b = grad_residual.astype(BF)
    grad_dense_bias = jnp.sum(grad_residual, axis=0)

    context_t = context
    res_halves = grad_res_b.reshape(rows, 2, half)
    res_keep = lax.dynamic_index_in_dim(res_halves, core, 1, keepdims=False)
    res_give = lax.dynamic_index_in_dim(res_halves, 1 - core, 1, keepdims=False)
    dense_sum = dot_tn(context_t, res_keep) + at.to_core(dot_tn(context_t, res_give).astype(BF)).astype(F32)

    def dense_terms(k):
        z = lax.rem(at.z + k, nz)
        return lax.dynamic_slice_in_dim(dense_sum, z * nx * rd, nx * rd, 0).reshape(nx, rd, half)

    dense_total = at.scatter_xz(dense_terms)

    grad_context = dot_nt(grad_res_b, wd).astype(BF).reshape(rows, 2, half)
    gc_keep = lax.dynamic_index_in_dim(grad_context, core, 1, keepdims=False)
    gc_give = lax.dynamic_index_in_dim(grad_context, 1 - core, 1, keepdims=False)
    grad_ctx = jnp.stack([gc_keep, at.to_core(gc_give)]).reshape(2, rows, heads, hd)
    grad_probs = jnp.einsum("bqhd,bkhd->bhqk", grad_ctx, values, preferred_element_type=F32)
    grad_scores = probs * (grad_probs - jnp.sum(probs * grad_probs, axis=-1, keepdims=True)) * hd ** (-0.5)
    grad_scores = grad_scores.astype(BF)
    grad_q = jnp.einsum("bhqk,bkhd->bqhd", grad_scores, keys, preferred_element_type=F32).reshape(2 * rows, half)
    grad_k = jnp.einsum("bhqk,bqhd->bkhd", grad_scores, queries, preferred_element_type=F32).reshape(2 * rows, half)
    grad_v = jnp.einsum("bhqk,bqhd->bkhd", probs_b, grad_ctx, preferred_element_type=F32).reshape(2 * rows, half)
    grad_q_bias, grad_v_bias = jnp.sum(grad_q, axis=0), jnp.sum(grad_v, axis=0)
    grad_qkv_b = jnp.concatenate([grad_q, grad_k, grad_v], axis=1).astype(BF)

    cols = 3 * half // 2
    pre_y = lax.dynamic_slice_in_dim(grad_qkv_b, y * cols, cols, 1)
    pre_n = lax.dynamic_slice_in_dim(grad_qkv_b, (1 - y) * cols, cols, 1)

    def qkv_terms(columns):
        return lambda k: dot_tn(owner_cols(normed_in, k, rd), columns).reshape(nx, rd, cols)

    qkv_own, qkv_other = at.scatter_yxz(qkv_terms(pre_n), qkv_terms(pre_y))
    gnorm = dot_nt(grad_qkv_b, wq)
    grad_normed = gnorm[:rows] + at.to_core(gnorm[rows:])
    grad_ln1_gain = jnp.sum(grad_normed * normed_one, axis=0)
    grad_ln1_bias = jnp.sum(grad_normed, axis=0)
    input_grad = grad_residual + norm_back(grad_normed * gain1, normed_one, inv_one)

    down_y = jnp.concatenate(pick(down_own, down_other, y), axis=0)
    grad_down = jnp.concatenate(pick(down_y, at.to_core(down_y), core), axis=0).astype(F32)
    up_c = up_total.reshape(rd, 2, shards, quarter).transpose(0, 2, 1, 3).reshape(rd, shards, 1, 2 * quarter)
    grad_up = jnp.concatenate(pick(up_c, at.to_core(up_c), core), axis=2).reshape(rd, ff)
    grad_dense = jnp.concatenate(pick(dense_total, at.to_core(dense_total), core), axis=1)
    qkv_c = jnp.concatenate(pick(qkv_own, qkv_other, y), axis=1).reshape(rd, 3, 1, half)
    grad_qkv = jnp.concatenate(pick(qkv_c, at.to_core(qkv_c), core), axis=2).reshape(rd, 3 * width).astype(F32)

    up_y = jnp.stack([g.reshape(shards, quarter) for g in pick(grad_up_bias[0], grad_up_bias[1], y)], axis=1)
    on_core = jnp.arange(2) == core
    up_bias_all = jnp.where(on_core[None, :, None, None], up_y[:, None], 0.0).reshape(-1)
    feed = jnp.concatenate([grad_ln2_gain, grad_ln2_bias, up_bias_all, grad_down_bias, grad_dense_bias])
    feed = at.sum_all(feed[None, :])[0]
    qv_all = jnp.stack([grad_q_bias, grad_v_bias])
    qv_all = jnp.where(on_core[None, :, None], qv_all[:, None], 0.0).reshape(-1)
    attn = jnp.concatenate([grad_ln1_gain, grad_ln1_bias, qv_all])
    attn = at.sum_all(attn[None, :])[0]

    def own(vector, start, size):
        per = size // shards
        return lax.dynamic_slice_in_dim(vector, start + at.shard * per, per)

    return (
        output,
        input_grad,
        own(attn, 0, width),
        own(attn, width, width),
        grad_qkv,
        own(attn, 2 * width, 2 * width),
        grad_dense,
        own(feed, 3 * width + ff, width),
        own(feed, 0, width),
        own(feed, width, width),
        grad_up,
        own(feed, 2 * width, ff),
        grad_down,
        own(feed, 2 * width + ff, width),
    )


def solution(mesh):
    both, rows, vector = P(("rep", "shard"), None), P("shard", None), P("shard")
    weights = (vector, vector, rows, vector, rows, vector, vector, vector, rows, vector, rows, vector)
    return jax.shard_map(
        functools.partial(on_device, mesh.shape["rep"], mesh.shape["shard"]),
        mesh=mesh,
        in_specs=(both, both) + weights,
        out_specs=(both, both) + weights,
        check_vma=False,
    )
```

```python
import functools
import math

import jax
import jax.numpy as jnp
import numpy as np
from jax import lax
from jax.experimental import pallas as pl
from jax.experimental.pallas import tpu as pltpu
from jax.sharding import PartitionSpec as P

H = 16
BF = jnp.bfloat16
F32 = jnp.float32
AXES = ("rep", "shard")
gelu_coef = math.sqrt(2.0 / math.pi)
VMEM_LIMIT = 60 * 2**20


class Place:
    def __init__(self, reps, shards):
        self.reps, self.shards = reps, shards
        self.nx = max(n for n in (1, 2, 4, 8) if shards % n == 0 and n * n <= shards)
        self.nz = nz = shards // self.nx
        rep, shard = lax.axis_index("rep"), lax.axis_index("shard")
        self.shard = shard
        self.slots = [(kz, kx) for kz in range(nz) for kx in range(self.nx)]
        table = np.zeros((reps * shards, 4 + 2 * shards), np.int32)
        for r in range(reps):
            for s in range(shards):
                y, core, z, x = r // 2, r % 2, s // self.nx, s % self.nx
                source = [(z - kz) % nz * self.nx + (x - kx) % self.nx for kz, kx in self.slots]
                in_half = [v - core * shards // 2 if v * 2 // shards == core else -1 for v in source]
                table[r * shards + s] = [y, core, z, x] + source + in_half
        row = lax.dynamic_slice_in_dim(jnp.asarray(table), rep * shards + shard, 1, 0)
        self.info = row[0]
        self.y, self.core, self.x = self.info[0], self.info[1], self.info[3]

    def _send(self, value, move, among=None):
        pairs = []
        for rep in range(self.reps):
            for shard in range(self.shards):
                here = (rep // 2, rep % 2, shard // self.nx, shard % self.nx)
                if among is None or among(*here):
                    y, core, z, x = move(*here)
                    pairs.append((rep * self.shards + shard, (y * 2 + core) * self.shards + z * self.nx + x))
        return lax.ppermute(value, AXES, pairs)

    def to_core(self, value):
        return self._send(value, lambda y, core, z, x: (y, 1 - core, z, x))

    def to_y(self, value):
        return self._send(value, lambda y, core, z, x: (1 - y, core, z, x))

    def to_z(self, value, k, among=None):
        return self._send(value, lambda y, core, z, x: (y, core, (z + k) % self.nz, x), among)

    def to_x(self, value, k, among=None):
        return self._send(value, lambda y, core, z, x: (y, core, z, (x + k) % self.nx), among)

    def gather(self, block, half=False):
        held_by_core = lambda core, z: z * 2 // self.nz == core
        held = [block] + [
            self.to_z(block, k, (lambda y, core, z, x: held_by_core(core, z)) if half else None)
            for k in range(1, self.nz)
        ]
        out = []
        for kz, value in enumerate(held):
            among = (lambda y, core, z, x, kz=kz: held_by_core(core, (z - kz) % self.nz)) if half else None
            out += [value] + [self.to_x(value, kx, among) for kx in range(1, self.nx)]
        return out

    def sum_all(self, value):
        value = value + self.to_core(value)
        value = value + self.to_y(value)
        value = sum([self.to_x(value, k) for k in range(1, self.nx)], value)
        return sum([self.to_z(value, k) for k in range(1, self.nz)], value)

    def z_groups(self):
        order = sorted(range(self.nz), key=lambda k: -min(k, self.nz - k))
        return order[: self.nz // 2], order[self.nz // 2 :]


def vmem():
    return pl.BlockSpec(memory_space=pltpu.VMEM)


def call(body, outs, ins, kinds, scratch=(), flops=0, name=None):
    spec = {
        "v": vmem(),
        "a": pl.BlockSpec(memory_space=pl.ANY),
        "s": pl.BlockSpec(memory_space=pltpu.SMEM),
    }
    moved = sum(v.size * v.dtype.itemsize for v in ins) + sum(math.prod(s) * jnp.dtype(t).itemsize for s, t in outs)
    return pl.pallas_call(
        body,
        out_shape=[jax.ShapeDtypeStruct(s, t) for s, t in outs],
        in_specs=[spec[k] for k in kinds],
        out_specs=[vmem() for _ in outs],
        scratch_shapes=list(scratch),
        compiler_params=pltpu.CompilerParams(vmem_limit_bytes=VMEM_LIMIT),
        cost_estimate=pl.CostEstimate(flops=flops, bytes_accessed=moved, transcendentals=0),
        name=name,
    )(*ins)


def dot(a, b):
    return jnp.dot(a, b, preferred_element_type=F32)


def dot_tn(a, b):
    return lax.dot_general(a, b, (((0,), (0,)), ((), ())), preferred_element_type=F32)


def dot_nt(a, b):
    return lax.dot_general(a, b, (((1,), (1,)), ((), ())), preferred_element_type=F32)


def layer_norm(values_in):
    centre = values_in - jnp.mean(values_in, axis=-1, keepdims=True)
    inv_std = lax.rsqrt(jnp.mean(centre * centre, axis=-1, keepdims=True) + 1e-05)
    return (centre * inv_std, inv_std)


def norm_back(grad_normed, normed, inv_std):
    return inv_std * (
        grad_normed
        - jnp.mean(grad_normed, axis=-1, keepdims=True)
        - normed * jnp.mean(grad_normed * normed, axis=-1, keepdims=True)
    )


def aligned(value, step):
    return pl.multiple_of(value, step) if step % 8 == 0 else value


def load_slots(slots, info, base, rows, target, sem, start):
    for i, slot in enumerate(slots):
        at = aligned(info[base + i] * rows, rows)
        copy = pltpu.make_async_copy(slot, target.at[pl.ds(at, rows), :], sem.at[i])
        if start:
            copy.start()
        else:
            copy.wait()


def load_half(slots, info, base, rows, target, sem, start):
    for i, slot in enumerate(slots):
        place = info[base + i]

        @pl.when(place >= 0)
        def _(i=i, slot=slot, place=place):
            at = aligned(place * rows, rows)
            copy = pltpu.make_async_copy(slot, target.at[pl.ds(at, rows), :], sem.at[i])
            if start:
                copy.start()
            else:
                copy.wait()


def load_down(slots, info, base, rows, target, sem, start):
    total = target.shape[0] // 2
    for i, slot in enumerate(slots):
        for part in range(2):
            half = jnp.bitwise_xor(info[0], part)
            at = aligned(half * total + info[base + i] * rows, rows)
            copy = pltpu.make_async_copy(
                slot.at[pl.ds(part * rows, rows), :], target.at[pl.ds(at, rows), :], sem.at[2 * i + part]
            )
            if start:
                copy.start()
            else:
                copy.wait()


def attention_kernel(n, rd, *refs):
    info, slopes, own, other, gain, bias, qv, *rest = refs
    slots, (nin_ref, qkv_ref, ctx_ref, probs_ref, wq, sem) = rest[:n], rest[n:]
    load_slots(slots, info, 4, rd, wq, sem, True)
    rows, width = own.shape
    half = width // 2
    for i, ref in enumerate((own, other)):
        normed, _ = layer_norm(ref[...].astype(F32))
        nin_ref[i * rows : (i + 1) * rows, :] = (normed * gain[...] + bias[...]).astype(BF)
    load_slots(slots, info, 4, rd, wq, sem, False)
    tile = 256

    @pl.loop(0, 3 * half // tile)
    def _(t):
        cols = pl.ds(pl.multiple_of(t * tile, tile), tile)
        qkv_ref[:, cols] = (dot(nin_ref[...], wq[:, cols]) + qv[:, cols]).astype(BF)

    hd = width // H
    lane = lax.broadcasted_iota(jnp.int32, (rows, 2 * hd), 1)
    first = lane < hd
    q_pos = lax.broadcasted_iota(jnp.int32, (rows, rows), 0)
    k_pos = lax.broadcasted_iota(jnp.int32, (rows, rows), 1)
    distance = (k_pos - q_pos).astype(F32)
    seen = k_pos <= q_pos
    pairs = half // (2 * hd)

    @pl.loop(0, 2 * pairs)
    def _(step):
        seq, pair = step // pairs, step % pairs
        at = pl.ds(pl.multiple_of(seq * rows, rows), rows)
        lanes = [pl.ds(pl.multiple_of(part * half + pair * 2 * hd, 2 * hd), 2 * hd) for part in range(3)]
        q, k, v = (qkv_ref[at, where] for where in lanes)
        out = []
        for i in range(2):
            mine = first if i == 0 else jnp.logical_not(first)
            scores = dot_nt(jnp.where(mine, q, jnp.zeros_like(q)), k) * hd ** (-0.5) + slopes[pair * 2 + i] * distance
            scores = jnp.where(seen, scores, -1e30)
            e = jnp.exp(scores - jnp.max(scores, axis=-1, keepdims=True))
            probs = (e * (1.0 / jnp.sum(e, axis=-1, keepdims=True))).astype(BF)
            probs_ref[step * 2 + i] = probs
            out.append(dot(probs, v))
        ctx_ref[at, lanes[0]] = jnp.where(first, out[0], out[1]).astype(BF)


def dense_kernel(n, rd, *refs):
    info, ctx, *rest = refs
    slots, (out_ref, wd, sem) = rest[:n], rest[n:]
    load_half(slots, info, 4 + n, rd, wd, sem, True)
    load_half(slots, info, 4 + n, rd, wd, sem, False)
    out_ref[...] = dot(ctx[...], wd[...])


def middle_kernel(own, other, part, recv, dense_b, gain, bias, res_ref, mid_ref):
    rows = own.shape[0]
    for i, ref in enumerate((own, other)):
        here, there = slice(i * rows, (i + 1) * rows), slice((1 - i) * rows, (2 - i) * rows)
        residual = ref[...].astype(F32) + (part[here, :] + recv[there, :]) + dense_b[...]
        res_ref[here, :] = residual
        normed, _ = layer_norm(residual)
        mid_ref[here, :] = (normed * gain[...] + bias[...]).astype(BF)


def up_kernel(n, rd, *refs):
    info, mid, up_b, *rest = refs
    slots, (act_ref, slope_ref, wu, sem) = rest[: 2 * n], rest[2 * n :]
    cols = slots[0].shape[1]
    for start in (True, False):
        for j in range(2):
            load_slots(
                slots[j * n : (j + 1) * n], info, 4, rd, wu.at[:, pl.ds(j * cols, cols)], sem.at[pl.ds(j * n, n)], start
            )
    tile = 256

    @pl.loop(0, 2 * cols // tile)
    def _(t):
        at = pl.ds(pl.multiple_of(t * tile, tile), tile)
        u = dot(mid[...], wu[:, at]) + up_b[:, at]
        t_ = jnp.tanh(gelu_coef * (u + 0.044715 * u * u * u))
        act_ref[:, at] = (0.5 * u * (1.0 + t_)).astype(BF)
        slope_ref[:, at] = 0.5 * (1.0 + t_) + 0.5 * u * (1.0 - t_ * t_) * gelu_coef * (
            1.0 + 3.0 * 0.044715 * u * u
        )


def feed_back_kernel(n, rd, quarter, *refs):
    info, own, other, slope, *rest = refs
    up_slots, down_slots, (gp_ref, gb_ref, gmid_ref, wu, wo, sem, sem2) = rest[: 2 * n], rest[2 * n : 3 * n], rest[3 * n :]
    cols = up_slots[0].shape[1]
    for start in (True, False):
        load_down(down_slots, info, 4, quarter, wo, sem2, start)
        for j in range(2):
            load_slots(
                up_slots[j * n : (j + 1) * n],
                info,
                4,
                rd,
                wu.at[:, pl.ds(j * cols, cols)],
                sem.at[pl.ds(j * n, n)],
                start,
            )
    rows = own.shape[0]
    tile = 256

    @pl.loop(0, 2 * cols // tile)
    def _(t):
        at = pl.ds(pl.multiple_of(t * tile, tile), tile)
        total = jnp.zeros((1, tile), F32)
        for i, ref in enumerate((own, other)):
            here = slice(i * rows, (i + 1) * rows)
            grad_pre = dot_nt(ref[...], wo[at, :]) * slope[here, at]
            gp_ref[here, at] = grad_pre.astype(BF)
            total = total + jnp.sum(grad_pre, axis=0, keepdims=True)
        gb_ref[:, at] = total

    width = own.shape[1]

    @pl.loop(0, width // tile)
    def _(t):
        at = pl.ds(pl.multiple_of(t * tile, tile), tile)
        gmid_ref[:, at] = dot_nt(gp_ref[...], wu[at, :])


def output_kernel(n, quarter, *refs):
    info, act, *rest = refs
    slots, (own_ref, other_ref, wo, sem) = rest[:n], rest[n:]
    for start in (True, False):
        load_down(slots, info, 4, quarter, wo, sem, start)
    rows, width = own_ref.shape
    tile = 256

    @pl.loop(0, width // tile)
    def _(t):
        at = pl.ds(pl.multiple_of(t * tile, tile), tile)
        both = dot(act[...], wo[:, at])
        own_ref[:, at] = both[:rows]
        other_ref[:, at] = both[rows:]


def owner_lanes(info, k, nz, size, base=0):
    return pl.ds(pl.multiple_of(base + lax.rem(info[2] + k, nz) * size, 128), size)


def grad_y_kernel(groups, nz, size, bases, by_y, info, left, *refs):
    right, outs = refs[: -2 * len(groups)], refs[-2 * len(groups) :]
    rows = right[0].shape[0]
    for g, ks in enumerate(groups):
        for j, k in enumerate(ks):
            for which in range(2):
                out = outs[2 * g + which]
                total = None
                for i, ref in enumerate(right):
                    here = slice(i * rows, (i + 1) * rows)
                    if by_y:
                        cols = out.shape[-1]
                        y = info[0] if which == 1 else 1 - info[0]
                        value = ref[:, pl.ds(pl.multiple_of(y * cols, 128), cols)]
                        lhs = left[here, owner_lanes(info, k, nz, size)]
                    else:
                        value = ref[...]
                        lhs = left[here, owner_lanes(info, k, nz, size, bases[1 - which])]
                    term = dot_tn(lhs, value)
                    total = term if total is None else total + term
                out[j] = total.astype(BF)


def grad_x_kernel(ks_groups, nz, nx, per, swap, info, left, right, *outs):
    size = nx * per
    for g, ks in enumerate(ks_groups):
        for j, k in enumerate(ks):
            for kx in range(nx):
                x = lax.rem(info[3] + kx, nx)
                out = outs[g * nx + kx]
                if nx * per % 128 == 0 and per % 128 == 0:
                    lanes = pl.ds(pl.multiple_of(lax.rem(info[2] + k, nz) * size + x * per, 128), per)
                    lhs = left[:, lanes]
                    rows = slice(None)
                else:
                    lhs = left[:, owner_lanes(info, k, nz, size)]
                    rows = None
                cols = right.shape[1] // 2
                for half in range(2):
                    value = dot_tn(lhs, right[:, half * cols : (half + 1) * cols]).astype(BF)
                    if rows is None:
                        picked = value[:per]
                        for v in range(1, nx):
                            picked = jnp.where(x == v, value[v * per : (v + 1) * per], picked)
                        value = picked
                    at = jnp.bitwise_xor(info[0], half) if swap else half
                    out[j, :, pl.ds(pl.multiple_of(at * cols, 128), cols)] = value


def fold_y_kernel(nx, per, info, mine, recv, *outs):
    for kx in range(nx):
        x = lax.rem(info[3] + kx, nx)
        at = pl.ds(aligned(x * per, per), per)
        outs[kx][...] = (mine[:, at, :].astype(F32) + recv[:, at, :].astype(F32)).astype(BF)


def fold_x_kernel(count, *refs):
    ins, outs = refs[:count], refs[count:]
    for j, out in enumerate(outs):
        out[...] = sum(ref[j].astype(F32) for ref in ins).astype(BF)


def sum_kernel(*refs):
    refs[-1][...] = sum(ref[...].astype(F32) for ref in refs[:-1]).astype(BF)


def attention_back_kernel(n, rd, *refs):
    info, part, recv, residual, own, other, gain, qkv, probs, *rest = refs
    slots, outs = rest[:n], rest[n:]
    res_ref, resb_ref, sums_ref, dqkv_ref, qvb_ref, wd, gctx, sem = outs
    load_half(slots, info, 4 + n, rd, wd, sem, True)
    rows, width = own.shape
    half = width // 2
    hd = width // H
    for i, ref in enumerate((own, other)):
        here, there = slice(i * rows, (i + 1) * rows), slice((1 - i) * rows, (2 - i) * rows)
        grad_mid = part[here, :] + recv[there, :]
        normed, inv_std = layer_norm(residual[here, :])
        grad_res = ref[...].astype(F32) + norm_back(grad_mid * gain[...], normed, inv_std)
        resb_ref[here, :] = grad_res.astype(BF)
        if i == 0:
            res_ref[...] = grad_res
            sums_ref[0:1, :] = jnp.sum(grad_mid * normed, axis=0, keepdims=True)
            sums_ref[1:2, :] = jnp.sum(grad_mid, axis=0, keepdims=True)
            sums_ref[2:3, :] = jnp.sum(grad_res, axis=0, keepdims=True)
    load_half(slots, info, 4 + n, rd, wd, sem, False)
    gctx[...] = dot_nt(resb_ref[...], wd[...]).astype(BF)

    lane = lax.broadcasted_iota(jnp.int32, (rows, 2 * hd), 1)
    first = lane < hd
    pairs = half // (2 * hd)
    qvb_ref[...] = jnp.zeros_like(qvb_ref)

    @pl.loop(0, 2 * pairs)
    def _(step):
        seq, pair = step // pairs, step % pairs
        at = pl.ds(pl.multiple_of(seq * rows, rows), rows)
        lanes = [pl.ds(pl.multiple_of(p * half + pair * 2 * hd, 2 * hd), 2 * hd) for p in range(3)]
        q, k, v = (qkv[at, where] for where in lanes)
        g = gctx[at, lanes[0]]
        dq, dk, dv = 0.0, 0.0, 0.0
        for i in range(2):
            mine = first if i == 0 else jnp.logical_not(first)
            g_i = jnp.where(mine, g, jnp.zeros_like(g))
            prob = probs[step * 2 + i]
            prob_f = prob.astype(F32)
            grad_probs = dot_nt(g_i, v)
            delta = jnp.sum(prob_f * grad_probs, axis=-1, keepdims=True)
            grad_scores = (prob_f * (grad_probs - delta) * hd ** (-0.5)).astype(BF)
            dq = dq + dot(grad_scores, jnp.where(mine, k, jnp.zeros_like(k)))
            dk = dk + dot_tn(grad_scores, jnp.where(mine, q, jnp.zeros_like(q)))
            dv = dv + dot_tn(prob, g_i)
        for where, value in zip(lanes, (dq, dk, dv)):
            dqkv_ref[at, where] = value.astype(BF)
        for row, value in ((0, dq), (1, dv)):
            qvb_ref[row : row + 1, lanes[0]] = qvb_ref[row : row + 1, lanes[0]] + jnp.sum(value, axis=0, keepdims=True)


def normed_kernel(n, rd, *refs):
    info, dqkv, *rest = refs
    slots, (own_ref, other_ref, wq, sem) = rest[:n], rest[n:]
    for start in (True, False):
        load_slots(slots, info, 4, rd, wq, sem, start)
    rows, width = own_ref.shape
    tile = 256

    @pl.loop(0, width // tile)
    def _(t):
        at = pl.ds(pl.multiple_of(t * tile, tile), tile)
        both = dot_nt(dqkv[...], wq[at, :])
        own_ref[:, at] = both[:rows]
        other_ref[:, at] = both[rows:]


def input_kernel(own, recv, hidden, grad_res, gain, in_ref, sums_ref):
    grad_normed = own[...] + recv[...]
    normed, inv_std = layer_norm(hidden[...].astype(F32))
    sums_ref[0:1, :] = jnp.sum(grad_normed * normed, axis=0, keepdims=True)
    sums_ref[1:2, :] = jnp.sum(grad_normed, axis=0, keepdims=True)
    in_ref[...] = grad_res[...] + norm_back(grad_normed * gain[...], normed, inv_std)


def pick(pair_first, pair_second, index):
    flip = index == 1
    return jnp.where(flip, pair_second, pair_first), jnp.where(flip, pair_first, pair_second)


def on_device(
    reps,
    shards,
    hidden_in,
    cotangent,
    ln1_gain,
    ln1_bias,
    w_qkv,
    qv_bias,
    w_dense,
    dense_bias,
    ln2_gain,
    ln2_bias,
    w_up,
    up_bias,
    w_down,
    down_bias,
):
    at = Place(reps, shards)
    info, core, y = at.info, at.core, at.y
    nz, nx, n = at.nz, at.nx, shards
    rows, width = hidden_in.shape
    rd = w_qkv.shape[0]
    ff = w_up.shape[1]
    quarter = ff // shards // 4
    half = width // 2
    heads = H // 2
    hd = width // H
    fq = shards * quarter
    dma = pltpu.SemaphoreType.DMA
    slopes = jnp.asarray(2.0 ** (-8.0 * (np.arange(H) + 1.0) / H), F32)
    slopes = lax.dynamic_slice_in_dim(slopes, core * heads, heads)

    qkv_half = lax.dynamic_index_in_dim(w_qkv.reshape(rd, 3, 2, half), core, 2, keepdims=False)
    qkv_slots = at.gather(qkv_half.reshape(rd, 3 * half))
    hidden_other = at.to_core(hidden_in)

    vectors = (ln1_gain, ln1_bias, qv_bias, dense_bias, ln2_gain, ln2_bias, up_bias, down_bias)
    packed = jnp.concatenate(vectors).astype(F32)[None, :]
    held = jnp.concatenate([packed] + [at.to_z(packed, k) for k in range(1, nz)])
    held = jnp.stack([held] + [at.to_x(held, k) for k in range(1, nx)], axis=1).reshape(n, -1)
    placed = info[4 : 4 + n][None, :] == jnp.arange(n)[:, None]
    packed = jnp.sum(jnp.where(placed[:, :, None], held[None], 0.0), axis=1)
    whole, start = [], 0
    for v in vectors:
        whole.append(packed[:, start : start + v.shape[0]].reshape(1, -1))
        start += v.shape[0]
    gain1, bias1, qv_b, dense_b, gain2, bias2, up_b, down_b = whole
    qv_half = lax.dynamic_index_in_dim(qv_b.reshape(2, 2, half), core, 1, keepdims=False)
    qkv_bias = jnp.concatenate([qv_half[:1], jnp.zeros((1, half), F32), qv_half[1:]], axis=1)
    up_b4 = lax.dynamic_index_in_dim(up_b.reshape(n, 2, 2, quarter), core, 1, keepdims=False)
    up_halves = jnp.concatenate(pick(up_b4[:, 0].reshape(1, -1), up_b4[:, 1].reshape(1, -1), y), axis=1)

    dense_slots = at.gather(w_dense, half=True)
    up_quarter = w_up.reshape(rd, n, 4, quarter)
    up_quarter = lax.dynamic_index_in_dim(up_quarter, core * 2 + y, 2, keepdims=False).reshape(rd, fq)
    up_slots = at.gather(up_quarter)
    up_slots = up_slots + [at.to_y(v) for v in up_slots]
    down_slots = at.gather(lax.dynamic_slice_in_dim(w_down, core * 2 * quarter, 2 * quarter, 0))
    cot_other = at.to_core(cotangent)

    mac = 2 * 2 * rows * width
    nin, qkv, ctx, probs = call(
        functools.partial(attention_kernel, n, rd),
        [((2 * rows, width), BF), ((2 * rows, 3 * half), BF), ((2 * rows, half), BF), ((2 * heads, rows, rows), BF)],
        [info, slopes, hidden_in, hidden_other, gain1, bias1, qkv_bias] + qkv_slots,
        "ss" + "v" * 5 + "a" * n,
        [pltpu.VMEM((width, 3 * half), BF), dma((n,))],
        mac * 4 * half,
        "attn",
    )
    (part,) = call(
        functools.partial(dense_kernel, n, rd),
        [((2 * rows, width), F32)],
        [info, ctx] + dense_slots,
        "sv" + "a" * n,
        [pltpu.VMEM((half, width), BF), dma((n,))],
        mac * half,
        "dense",
    )
    residual, mid = call(
        middle_kernel,
        [((2 * rows, width), F32), ((2 * rows, width), BF)],
        [hidden_in, hidden_other, part, at.to_core(part), dense_b, gain2, bias2],
        "v" * 7,
        name="middle",
    )
    act, slope = call(
        functools.partial(up_kernel, n, rd),
        [((2 * rows, 2 * fq), BF), ((2 * rows, 2 * fq), F32)],
        [info, mid, up_halves] + up_slots,
        "svv" + "a" * 2 * n,
        [pltpu.VMEM((width, 2 * fq), BF), dma((2 * n,))],
        mac * 2 * fq,
        "up",
    )

    groups = at.z_groups()

    def scatter_y(left, right, per, cols, bases, by_y, name):
        outs = [((len(ks), nx * per, cols), BF) for ks in groups for _ in range(2)]
        terms = call(
            functools.partial(grad_y_kernel, groups, nz, nx * per, bases, by_y),
            outs,
            [info, left] + right,
            "sv" + "v" * len(right),
            flops=mac * n * per * cols // width * 2,
            name=name,
        )
        sent = []
        for g, ks in enumerate(groups):
            away, mine = terms[2 * g], terms[2 * g + 1]
            parts = call(
                functools.partial(fold_y_kernel, nx, per),
                [((len(ks), per, cols), BF)] * nx,
                [info, mine, at.to_y(away)],
                "svv",
                name=name + "_y",
            )
            sent.append(parts)
        own = over_xz(sent, per, cols, name)
        return own, at.to_y(own)

    def over_xz(parts_of, per, cols, name):
        terms = []
        for ks, parts in zip(groups, parts_of):
            ins = [parts[0]] + [at.to_x(parts[kx], kx) for kx in range(1, nx)]
            sums = call(
                functools.partial(fold_x_kernel, nx),
                [((per, cols), BF)] * len(ks),
                ins,
                "v" * nx,
                name=name + "_x",
            )
            terms += [v if k == 0 else at.to_z(v, k) for k, v in zip(ks, sums)]
        return call(sum_kernel, [((per, cols), BF)], terms, "v" * nz, name=name + "_z")[0]

    def terms_x(left, right, per, cols, swap, name):
        outs = [((len(ks), per, cols), BF) for ks in groups for _ in range(nx)]
        terms = call(
            functools.partial(grad_x_kernel, groups, nz, nx, per, swap),
            outs,
            [info, left, right],
            "svv",
            flops=mac * n * per * cols // width,
            name=name,
        )
        return [terms[g * nx : (g + 1) * nx] for g in range(len(groups))]

    down_own, down_other = scatter_y(act, [cotangent, cot_other], quarter, width, (0, fq), False, "gdown")

    gpre, gpre_sums, gmid = call(
        functools.partial(feed_back_kernel, n, rd, quarter),
        [((2 * rows, 2 * fq), BF), ((1, 2 * fq), F32), ((2 * rows, width), F32)],
        [info, cotangent, cot_other, slope] + up_slots + down_slots,
        "svvv" + "a" * 3 * n,
        [pltpu.VMEM((width, 2 * fq), BF), pltpu.VMEM((2 * fq, width), BF), dma((2 * n,)), dma((2 * n,))],
        mac * 4 * fq,
        "feed_back",
    )
    gmid_recv = at.to_core(gmid)
    up_part = over_xz(terms_x(mid, gpre, rd, 2 * fq, True, "gup"), rd, 2 * fq, "gup")
    up_recv = at.to_y(up_part)

    grad_res, grad_res_b, sums2, dqkv, qv_sums = call(
        functools.partial(attention_back_kernel, n, rd),
        [
            ((rows, width), F32),
            ((2 * rows, width), BF),
            ((3, width), F32),
            ((2 * rows, 3 * half), BF),
            ((2, half), F32),
        ],
        [info, gmid, gmid_recv, residual, cotangent, cot_other, gain2, qkv, probs] + dense_slots,
        "s" + "v" * 8 + "a" * n,
        [pltpu.VMEM((half, width), BF), pltpu.VMEM((2 * rows, half), BF), dma((n,))],
        mac * 3 * half,
        "attn_back",
    )
    qkv_own, qkv_other = scatter_y(nin, [dqkv], rd, 3 * half // 2, None, True, "gqkv")

    def dense_terms(info_, left, right, *outs):
        for j in range(nz // 2):
            for kx in range(nx):
                x = lax.rem(info_[3] + kx, nx)
                if rd % 128 == 0:
                    lhs = left[:, pl.ds(pl.multiple_of((j * nx + x) * rd, 128), rd)]
                    outs[kx][j] = dot_tn(lhs, right[...]).astype(BF)
                else:
                    value = dot_tn(left[:, j * nx * rd : (j + 1) * nx * rd], right[...]).astype(BF)
                    picked = value[:rd]
                    for v in range(1, nx):
                        picked = jnp.where(x == v, value[v * rd : (v + 1) * rd], picked)
                    outs[kx][j] = picked

    dparts = call(
        dense_terms,
        [((nz // 2, rd, width), BF)] * nx,
        [info, ctx, grad_res_b],
        "svv",
        flops=mac * half,
        name="gdense",
    )
    dins = [dparts[0]] + [at.to_x(dparts[kx], kx) for kx in range(1, nx)]

    def dense_fold(info_, *refs):
        ins, outs = refs[:nx], refs[nx:]
        for k, out in enumerate(outs):
            place = lax.rem(info_[2] + k, nz) - info_[1] * (nz // 2)
            safe = jnp.clip(place, 0, nz // 2 - 1)
            out[...] = sum(ref[safe].astype(F32) for ref in ins).astype(BF)

    dsums = call(dense_fold, [((rd, width), BF)] * nz, [info] + dins, "s" + "v" * nx, name="gdense_x")
    toward = lambda k: lambda y, core, z, x: ((z + k) % nz) * 2 // nz == core
    dterms = [dsums[0]] + [at.to_z(dsums[k], k, toward(k)) for k in range(1, nz)]
    (dense_part,) = call(sum_kernel, [((rd, width), BF)], dterms, "v" * nz, name="gdense_z")
    dense_mine = dense_part.astype(F32) + at.to_y(dense_part).astype(F32)
    dense_recv = at.to_core(dense_mine)
    grad_dense = jnp.where(info[2] * 2 // nz == core, dense_mine, dense_recv)

    out_own, out_other = call(
        functools.partial(output_kernel, n, quarter),
        [((rows, width), F32), ((rows, width), F32)],
        [info, act] + down_slots,
        "sv" + "a" * n,
        [pltpu.VMEM((2 * fq, width), BF), dma((2 * n,))],
        mac * 2 * fq,
        "output",
    )
    output = (residual[:rows] + (out_own + at.to_core(out_other)) + down_b).astype(BF)

    norm_own, norm_other = call(
        functools.partial(normed_kernel, n, rd),
        [((rows, width), F32), ((rows, width), F32)],
        [info, dqkv] + qkv_slots,
        "sv" + "a" * n,
        [pltpu.VMEM((width, 3 * half), BF), dma((n,))],
        mac * 3 * half,
        "gnorm",
    )
    input_grad, sums1 = call(
        input_kernel,
        [((rows, width), F32), ((2, width), F32)],
        [norm_own, at.to_core(norm_other), hidden_in, grad_res, gain1],
        "v" * 5,
        name="input_grad",
    )

    down_y = jnp.concatenate(pick(down_own, down_other, y), axis=0)
    grad_down = jnp.concatenate(pick(down_y, at.to_core(down_y), core), axis=0).astype(F32)
    up_total = up_part.astype(F32) + up_recv.astype(F32)
    up_c = up_total.reshape(rd, 2, n, quarter).transpose(0, 2, 1, 3).reshape(rd, n, 1, 2 * quarter)
    grad_up = jnp.concatenate(pick(up_c, at.to_core(up_c), core), axis=2).reshape(rd, ff)
    qkv_c = jnp.concatenate(pick(qkv_own, qkv_other, y), axis=1).reshape(rd, 3, 1, half)
    grad_qkv = jnp.concatenate(pick(qkv_c, at.to_core(qkv_c), core), axis=2).reshape(rd, 3 * width).astype(F32)

    grad_down_bias = jnp.sum(cotangent.astype(F32), axis=0)
    up_y = jnp.stack([g.reshape(n, quarter) for g in pick(gpre_sums[0, :fq], gpre_sums[0, fq:], y)], axis=1)
    on_core = jnp.arange(2) == core
    up_bias_all = jnp.where(on_core[None, :, None, None], up_y[:, None], 0.0).reshape(-1)
    qv_all = jnp.where(on_core[None, :, None], qv_sums[:, None], 0.0).reshape(-1)
    feed = jnp.concatenate([sums2.reshape(-1), grad_down_bias, up_bias_all, sums1.reshape(-1), qv_all])
    feed = at.sum_all(feed[None, :])[0]

    def own(start, size):
        per = size // n
        return lax.dynamic_slice_in_dim(feed, start + at.shard * per, per)

    return (
        output,
        input_grad,
        own(4 * width + ff, width),
        own(5 * width + ff, width),
        grad_qkv,
        own(6 * width + ff, 2 * width),
        grad_dense,
        own(2 * width, width),
        own(0, width),
        own(width, width),
        grad_up,
        own(4 * width, ff),
        grad_down,
        own(3 * width, width),
    )


def solution(mesh):
    both, rows, vector = P(("rep", "shard"), None), P("shard", None), P("shard")
    weights = (vector, vector, rows, vector, rows, vector, vector, vector, rows, vector, rows, vector)
    return jax.shard_map(
        functools.partial(on_device, mesh.shape["rep"], mesh.shape["shard"]),
        mesh=mesh,
        in_specs=(both, both) + weights,
        out_specs=(both, both) + weights,
        check_vma=False,
    )
```

```python
import functools
import math

import jax
import jax.numpy as jnp
import numpy as np
from jax import lax
from jax.experimental import pallas as pl
from jax.experimental.pallas import tpu as pltpu
from jax.sharding import PartitionSpec as P

H = 16
BF = jnp.bfloat16
F32 = jnp.float32
AXES = ("rep", "shard")
gelu_coef = math.sqrt(2.0 / math.pi)
VMEM_LIMIT = 60 * 2**20


class Place:
    def __init__(self, reps, shards):
        self.reps, self.shards = reps, shards
        self.nx = max(n for n in (1, 2, 4, 8) if shards % n == 0 and n * n <= shards)
        self.nz = shards // self.nx
        rep, shard = lax.axis_index("rep"), lax.axis_index("shard")
        self.shard, self.waits = shard, [[]]
        table = [
            [r // 2, r % 2, v // self.nx, v % self.nx] for r in range(reps) for v in range(shards)
        ]
        row = lax.dynamic_slice_in_dim(jnp.asarray(np.array(table, np.int32)), rep * shards + shard, 1, 0)
        self.info = row[0]
        self.y, self.core, self.x = self.info[0], self.info[1], self.info[3]

    def _send(self, value, move):
        pairs = []
        for rep in range(self.reps):
            for shard in range(self.shards):
                y, core, z, x = move(rep // 2, rep % 2, shard // self.nx, shard % self.nx)
                pairs.append((rep * self.shards + shard, (y * 2 + core) * self.shards + z * self.nx + x))
        return lax.ppermute(value, AXES, pairs)

    def to_core(self, value):
        return self._send(value, lambda y, core, z, x: (y, 1 - core, z, x))

    def to_y(self, value):
        return self._send(value, lambda y, core, z, x: (1 - y, core, z, x))

    def to_z(self, value, k):
        return self._send(value, lambda y, core, z, x: (y, core, (z + k) % self.nz, x))

    def to_x(self, value, k):
        return self._send(value, lambda y, core, z, x: (y, core, z, (x + k) % self.nx))

    def swap_z(self, value):
        along = [[z * self.nx + x for z in range(self.nz)] for x in range(self.nx)]
        return lax.all_to_all(value, "shard", 0, 0, axis_index_groups=along, tiled=True)

    def gather(self, block, over_y=False):
        block = jnp.broadcast_to(block[None], (self.nz,) + block.shape)
        held = self.swap_z(after(block, self.waits.pop(0)))
        out = [held] + [self.to_x(held, kx) for kx in range(1, self.nx)]
        for i, values in enumerate(([held], out[1:])):
            self.hold(i, values)
        if over_y:
            out = out + [self.to_y(v) for v in out]
        return out

    def hold(self, steps, values):
        while len(self.waits) <= steps + 2:
            self.waits.append([])
        self.waits[steps] += values

    def sum_all(self, value):
        value = value + self.to_core(value)
        value = value + self.to_y(value)
        value = sum([self.to_x(value, k) for k in range(1, self.nx)], value)
        return sum([self.to_z(value, k) for k in range(1, self.nz)], value)


def after(value, waits):
    return lax.optimization_barrier((value, list(waits)))[0] if waits else value


def vmem():
    return pl.BlockSpec(memory_space=pltpu.VMEM)


def call(body, outs, ins, kinds, scratch=(), flops=0, name=None):
    spec = {
        "v": vmem(),
        "a": pl.BlockSpec(memory_space=pl.ANY),
        "s": pl.BlockSpec(memory_space=pltpu.SMEM),
    }
    moved = sum(v.size * v.dtype.itemsize for v in ins) + sum(math.prod(s) * jnp.dtype(t).itemsize for s, t in outs)
    return pl.pallas_call(
        body,
        out_shape=[jax.ShapeDtypeStruct(s, t) for s, t in outs],
        in_specs=[spec[k] for k in kinds],
        out_specs=[vmem() for _ in outs],
        scratch_shapes=list(scratch),
        compiler_params=pltpu.CompilerParams(vmem_limit_bytes=VMEM_LIMIT),
        cost_estimate=pl.CostEstimate(flops=10**12, bytes_accessed=10**9, transcendentals=0),
        name=name,
    )(*ins)


def dot(a, b):
    return jnp.dot(a, b, preferred_element_type=F32)


def dot_tn(a, b):
    return lax.dot_general(a, b, (((0,), (0,)), ((), ())), preferred_element_type=F32)


def dot_nt(a, b):
    return lax.dot_general(a, b, (((1,), (1,)), ((), ())), preferred_element_type=F32)


def layer_norm(values_in):
    centre = values_in - jnp.mean(values_in, axis=-1, keepdims=True)
    inv_std = lax.rsqrt(jnp.mean(centre * centre, axis=-1, keepdims=True) + 1e-05)
    return (centre * inv_std, inv_std)


def norm_back(grad_normed, normed, inv_std):
    return inv_std * (
        grad_normed
        - jnp.mean(grad_normed, axis=-1, keepdims=True)
        - normed * jnp.mean(grad_normed * normed, axis=-1, keepdims=True)
    )


def aligned(value, step):
    return pl.multiple_of(value, step) if step % 8 == 0 else value


class Load:
    def __init__(self, sem):
        self.sem, self.copies = sem, []

    def copy(self, source, target):
        self.copies.append(pltpu.make_async_copy(source, target, self.sem.at[len(self.copies)]))

    def start(self):
        for copy in self.copies:
            copy.start()

    def wait(self):
        for copy in self.copies:
            copy.wait()

    def blocks(self, info, held, rows, target, col, first=0, base=0):
        nx, nz, cols = len(held), held[0].shape[0], held[0].shape[2]
        for kx, ref in enumerate(held):
            x = lax.rem(info[3] - kx + nx, nx)
            for z in range(nz):
                at = aligned(base + (z * nx + x) * rows, rows)
                self.copy(ref.at[z, pl.ds(first, rows), :], target.at[pl.ds(at, rows), pl.ds(col, cols)])

    def qkv(self, info, pieces, rd, target):
        nx = len(pieces) // 2
        for i in range(2):
            self.blocks(info, pieces[i * nx : (i + 1) * nx], rd, target, i * pieces[0].shape[2])

    def dense(self, info, held, other, rd, target):
        nx, nz, cols = len(held), held[0].shape[0], held[0].shape[2]
        for kx, ref in enumerate(held):
            x = lax.rem(info[3] - kx + nx, nx)
            for j in range(nz // 2):
                rows = pl.ds(aligned((j * nx + x) * rd, rd), rd)
                for core, source in ((info[1], ref.at[info[1] * (nz // 2) + j]), (1 - info[1], other.at[kx, j])):
                    lanes = pl.ds(pl.multiple_of(core * cols, 128), cols)
                    self.copy(source, target.at[rows, lanes])

    def up(self, info, pieces, rd, target):
        nx = len(pieces) // 4
        for i in range(4):
            self.blocks(info, pieces[i * nx : (i + 1) * nx], rd, target, i * pieces[0].shape[2])

    def down(self, info, pieces, quarter, target):
        nx, half = len(pieces) // 3, target.shape[0] // 2
        self.blocks(info, pieces[:nx], quarter, target, 0)
        self.blocks(info, pieces[nx : 2 * nx], quarter, target, 0, base=half)
        for part in range(2):
            base = jnp.bitwise_xor(info[0], part) * half
            self.blocks(info, pieces[2 * nx :], quarter, target, pieces[0].shape[2], part * quarter, base)


def attention_kernel(n, rd, *refs):
    info, slopes, own, other, gain, bias, qv, *rest = refs
    pieces, (nin_ref, qkv_ref, ctx_ref, probs_ref, wq, sem) = rest[:n], rest[n:]
    load = Load(sem)
    load.qkv(info, pieces, rd, wq)
    load.start()
    rows, width = own.shape
    half = width // 2
    for i, ref in enumerate((own, other)):
        normed, _ = layer_norm(ref[...].astype(F32))
        nin_ref[i * rows : (i + 1) * rows, :] = (normed * gain[...] + bias[...]).astype(BF)
    load.wait()
    tile = 256

    @pl.loop(0, 3 * half // tile)
    def _(t):
        cols = pl.ds(pl.multiple_of(t * tile, tile), tile)
        qkv_ref[:, cols] = (dot(nin_ref[...], wq[:, cols]) + qv[:, cols]).astype(BF)

    hd = width // H
    lane = lax.broadcasted_iota(jnp.int32, (rows, 2 * hd), 1)
    first = lane < hd
    q_pos = lax.broadcasted_iota(jnp.int32, (rows, rows), 0)
    k_pos = lax.broadcasted_iota(jnp.int32, (rows, rows), 1)
    distance = (k_pos - q_pos).astype(F32)
    seen = k_pos <= q_pos
    pairs = half // (2 * hd)

    @pl.loop(0, 2 * pairs)
    def _(step):
        seq, pair = step // pairs, step % pairs
        at = pl.ds(pl.multiple_of(seq * rows, rows), rows)
        lanes = [pl.ds(pl.multiple_of(part * half + pair * 2 * hd, 2 * hd), 2 * hd) for part in range(3)]
        q, k, v = (qkv_ref[at, where] for where in lanes)
        out = []
        for i in range(2):
            mine = first if i == 0 else jnp.logical_not(first)
            scores = dot_nt(jnp.where(mine, q, jnp.zeros_like(q)), k) * hd ** (-0.5) + slopes[pair * 2 + i] * distance
            scores = jnp.where(seen, scores, -1e30)
            e = jnp.exp(scores - jnp.max(scores, axis=-1, keepdims=True))
            probs = (e * (1.0 / jnp.sum(e, axis=-1, keepdims=True))).astype(BF)
            probs_ref[step * 2 + i] = probs
            out.append(dot(probs, v))
        ctx_ref[at, lanes[0]] = jnp.where(first, out[0], out[1]).astype(BF)


def dense_kernel(n, rd, *refs):
    info, ctx, *rest = refs
    held, (other, out_ref, wd, sem) = rest[:n], rest[n:]
    load = Load(sem)
    load.dense(info, held, other, rd, wd)
    load.start()
    load.wait()
    out_ref[...] = dot(ctx[...], wd[...])


def middle_kernel(own, other, part, recv, dense_b, gain, bias, res_ref, mid_ref):
    rows = own.shape[0]
    for i, ref in enumerate((own, other)):
        here, there = slice(i * rows, (i + 1) * rows), slice((1 - i) * rows, (2 - i) * rows)
        residual = ref[...].astype(F32) + (part[here, :] + recv[there, :]) + dense_b[...]
        res_ref[here, :] = residual
        normed, _ = layer_norm(residual)
        mid_ref[here, :] = (normed * gain[...] + bias[...]).astype(BF)


def up_kernel(n, rd, *refs):
    info, mid, up_b, *rest = refs
    pieces, (act_ref, slope_ref, wu, sem) = rest[:n], rest[n:]
    load = Load(sem)
    load.up(info, pieces, rd, wu)
    load.start()
    cols = wu.shape[1] // 2
    load.wait()
    tile = 256

    @pl.loop(0, 2 * cols // tile)
    def _(t):
        at = pl.ds(pl.multiple_of(t * tile, tile), tile)
        u = dot(mid[...], wu[:, at]) + up_b[:, at]
        t_ = jnp.tanh(gelu_coef * (u + 0.044715 * u * u * u))
        act_ref[:, at] = (0.5 * u * (1.0 + t_)).astype(BF)
        slope_ref[:, at] = 0.5 * (1.0 + t_) + 0.5 * u * (1.0 - t_ * t_) * gelu_coef * (
            1.0 + 3.0 * 0.044715 * u * u
        )


def feed_back_kernel(n, rd, quarter, *refs):
    info, own, other, slope, *rest = refs
    up_pieces, down_pieces, (gp_ref, gb_ref, gmid_ref, wu, wo, sem, sem2) = rest[:n], rest[n : n + n // 4 * 3], rest[n + n // 4 * 3 :]
    load, load2 = Load(sem), Load(sem2)
    load.down(info, down_pieces, quarter, wo)
    load2.up(info, up_pieces, rd, wu)
    load.start()
    load2.start()
    load.wait()
    cols = wu.shape[1] // 2
    rows = own.shape[0]
    tile = 256

    @pl.loop(0, 2 * cols // tile)
    def _(t):
        at = pl.ds(pl.multiple_of(t * tile, tile), tile)
        total = jnp.zeros((1, tile), F32)
        for i, ref in enumerate((own, other)):
            here = slice(i * rows, (i + 1) * rows)
            grad_pre = dot_nt(ref[...], wo[at, :]) * slope[here, at]
            gp_ref[here, at] = grad_pre.astype(BF)
            total = total + jnp.sum(grad_pre, axis=0, keepdims=True)
        gb_ref[:, at] = total

    width = own.shape[1]
    load2.wait()

    @pl.loop(0, width // tile)
    def _(t):
        at = pl.ds(pl.multiple_of(t * tile, tile), tile)
        gmid_ref[:, at] = dot_nt(gp_ref[...], wu[at, :])


def output_kernel(n, quarter, *refs):
    info, act, *rest = refs
    pieces, (own_ref, other_ref, wo, sem) = rest[:n], rest[n:]
    load = Load(sem)
    load.down(info, pieces, quarter, wo)
    load.start()
    load.wait()
    rows, width = own_ref.shape
    tile = 256

    @pl.loop(0, width // tile)
    def _(t):
        at = pl.ds(pl.multiple_of(t * tile, tile), tile)
        both = dot(act[...], wo[:, at])
        own_ref[:, at] = both[:rows]
        other_ref[:, at] = both[rows:]


def grad_y_kernel(parts, by_y, info, left, *refs):
    right, outs = refs[: -2 * parts], refs[-2 * parts :]
    tokens = right[0].shape[0]
    nz, rows, cols = outs[0].shape
    for which in range(2):
        for p in range(parts):
            out = outs[2 * p + which]
            for z in range(nz):
                total = None
                for i, ref in enumerate(right):
                    here = slice(i * tokens, (i + 1) * tokens)
                    first, start = z * rows, p * cols
                    if by_y:
                        y = info[0] if which == 1 else 1 - info[0]
                        start = pl.multiple_of((y * parts + p) * cols, 128)
                    else:
                        first += (1 - which) * nz * rows
                    term = dot_tn(left[here, first : first + rows], ref[:, pl.ds(start, cols)])
                    total = term if total is None else total + term
                out[z] = total.astype(BF)


def at_x(info, kx, nx, per, value):
    x = lax.rem(info[3] + kx, nx)
    picked = value[:per]
    for v in range(1, nx):
        picked = jnp.where(x == v, value[v * per : (v + 1) * per], picked)
    return picked


def up_grad_kernel(nx, info, left, right, away, mine, *outs):
    nz, per, cols = outs[0].shape
    cols //= 2
    half = right.shape[1] // 2
    for z in range(nz):
        lhs = left[:, z * nx * per : (z + 1) * nx * per]
        for h in range(2):
            value = dot_tn(lhs, right[:, h * half : h * half + cols]).astype(BF)
            lanes = pl.ds(pl.multiple_of(jnp.bitwise_xor(info[0], h) * cols, 128), cols)
            for kx in range(nx):
                outs[kx][z, :, lanes] = at_x(info, kx, nx, per, value)
            out = away if h else mine
            out[z] = dot_tn(lhs, right[:, h * half + cols : (h + 1) * half]).astype(BF)


def fold_y_kernel(nx, info, mine, recv, *outs):
    per = outs[0].shape[1]
    for kx in range(nx):
        x = lax.rem(info[3] + kx, nx)
        at = pl.ds(aligned(x * per, per), per)
        outs[kx][...] = (mine[:, at, :].astype(F32) + recv[:, at, :].astype(F32)).astype(BF)


def dense_grad_kernel(info, left, right, keep, give):
    nz, rows, cols = keep.shape
    for z in range(nz):
        lhs = left[:, z * rows : (z + 1) * rows]
        for out, core in ((keep, info[1]), (give, 1 - info[1])):
            out[z] = dot_tn(lhs, right[:, pl.ds(pl.multiple_of(core * cols, 128), cols)]).astype(BF)


def dense_place_kernel(nx, info, mine, recv, *outs):
    nz, per = outs[0].shape[:2]
    for kx in range(nx):
        x = lax.rem(info[3] + kx, nx)
        at = pl.ds(aligned(x * per, per), per)
        outs[kx][pl.ds(info[1] * (nz // 2), nz // 2)] = mine[:, at, :]
        outs[kx][pl.ds((1 - info[1]) * (nz // 2), nz // 2)] = recv[:, at, :]


def total_kernel(*refs):
    out = refs[-1]
    at = 0
    for ref in refs[:-1]:
        cols = ref.shape[2]
        total = ref[0].astype(F32)
        for z in range(1, ref.shape[0]):
            total = total + ref[z].astype(F32)
        out[:, at : at + cols] = total.astype(BF)
        at += cols


def fold_x_kernel(nx, *refs):
    out = refs[-1]
    cols = refs[0].shape[2]
    for p in range(len(refs) // nx):
        total = refs[p * nx][...].astype(F32)
        for kx in range(1, nx):
            total = total + refs[p * nx + kx][...].astype(F32)
        out[:, :, p * cols : (p + 1) * cols] = total.astype(BF)


def attention_back_kernel(n, rd, *refs):
    info, part, recv, residual, own, other, gain, qkv, probs, *rest = refs
    held, outs = rest[:n], rest[n:]
    other_half, res_ref, resb_ref, sums_ref, dqkv_ref, qvb_ref, wd, gctx, sem = outs
    load = Load(sem)
    load.dense(info, held, other_half, rd, wd)
    load.start()
    rows, width = own.shape
    half = width // 2
    hd = width // H
    for i, ref in enumerate((own, other)):
        here, there = slice(i * rows, (i + 1) * rows), slice((1 - i) * rows, (2 - i) * rows)
        grad_mid = part[here, :] + recv[there, :]
        normed, inv_std = layer_norm(residual[here, :])
        grad_res = ref[...].astype(F32) + norm_back(grad_mid * gain[...], normed, inv_std)
        resb_ref[here, :] = grad_res.astype(BF)
        if i == 0:
            res_ref[...] = grad_res
            sums_ref[0:1, :] = jnp.sum(grad_mid * normed, axis=0, keepdims=True)
            sums_ref[1:2, :] = jnp.sum(grad_mid, axis=0, keepdims=True)
            sums_ref[2:3, :] = jnp.sum(grad_res, axis=0, keepdims=True)
    load.wait()
    gctx[...] = dot_nt(resb_ref[...], wd[...]).astype(BF)

    lane = lax.broadcasted_iota(jnp.int32, (rows, 2 * hd), 1)
    first = lane < hd
    pairs = half // (2 * hd)
    qvb_ref[...] = jnp.zeros_like(qvb_ref)

    @pl.loop(0, 2 * pairs)
    def _(step):
        seq, pair = step // pairs, step % pairs
        at = pl.ds(pl.multiple_of(seq * rows, rows), rows)
        lanes = [pl.ds(pl.multiple_of(p * half + pair * 2 * hd, 2 * hd), 2 * hd) for p in range(3)]
        q, k, v = (qkv[at, where] for where in lanes)
        g = gctx[at, lanes[0]]
        dq, dk, dv = 0.0, 0.0, 0.0
        for i in range(2):
            mine = first if i == 0 else jnp.logical_not(first)
            g_i = jnp.where(mine, g, jnp.zeros_like(g))
            prob = probs[step * 2 + i]
            prob_f = prob.astype(F32)
            grad_probs = dot_nt(g_i, v)
            delta = jnp.sum(prob_f * grad_probs, axis=-1, keepdims=True)
            grad_scores = (prob_f * (grad_probs - delta) * hd ** (-0.5)).astype(BF)
            dq = dq + dot(grad_scores, jnp.where(mine, k, jnp.zeros_like(k)))
            dk = dk + dot_tn(grad_scores, jnp.where(mine, q, jnp.zeros_like(q)))
            dv = dv + dot_tn(prob, g_i)
        for where, value in zip(lanes, (dq, dk, dv)):
            dqkv_ref[at, where] = value.astype(BF)
        for row, value in ((0, dq), (1, dv)):
            qvb_ref[row : row + 1, lanes[0]] = qvb_ref[row : row + 1, lanes[0]] + jnp.sum(value, axis=0, keepdims=True)


def normed_kernel(n, rd, *refs):
    info, dqkv, *rest = refs
    pieces, (own_ref, other_ref, wq, sem) = rest[:n], rest[n:]
    load = Load(sem)
    load.qkv(info, pieces, rd, wq)
    load.start()
    load.wait()
    rows, width = own_ref.shape
    tile = 256

    @pl.loop(0, width // tile)
    def _(t):
        at = pl.ds(pl.multiple_of(t * tile, tile), tile)
        both = dot_nt(dqkv[...], wq[at, :])
        own_ref[:, at] = both[:rows]
        other_ref[:, at] = both[rows:]


def input_kernel(own, recv, hidden, grad_res, gain, in_ref, sums_ref):
    grad_normed = own[...] + recv[...]
    normed, inv_std = layer_norm(hidden[...].astype(F32))
    sums_ref[0:1, :] = jnp.sum(grad_normed * normed, axis=0, keepdims=True)
    sums_ref[1:2, :] = jnp.sum(grad_normed, axis=0, keepdims=True)
    in_ref[...] = grad_res[...] + norm_back(grad_normed * gain[...], normed, inv_std)


def pick(pair_first, pair_second, index):
    flip = index == 1
    return jnp.where(flip, pair_second, pair_first), jnp.where(flip, pair_first, pair_second)


def on_device(
    reps,
    shards,
    hidden_in,
    cotangent,
    ln1_gain,
    ln1_bias,
    w_qkv,
    qv_bias,
    w_dense,
    dense_bias,
    ln2_gain,
    ln2_bias,
    w_up,
    up_bias,
    w_down,
    down_bias,
):
    at = Place(reps, shards)
    info, core, y = at.info, at.core, at.y
    nz, nx, n = at.nz, at.nx, shards
    rows, width = hidden_in.shape
    rd = w_qkv.shape[0]
    ff = w_up.shape[1]
    quarter = ff // shards // 4
    half = width // 2
    heads = H // 2
    hd = width // H
    fq = shards * quarter
    dma = pltpu.SemaphoreType.DMA
    slopes = jnp.asarray(2.0 ** (-8.0 * (np.arange(H) + 1.0) / H), F32)
    slopes = lax.dynamic_slice_in_dim(slopes, core * heads, heads)

    qkv_half = lax.dynamic_index_in_dim(w_qkv.reshape(rd, 3, 2, half), core, 2, keepdims=False)
    qkv_half = qkv_half.reshape(rd, 3 * half)
    cut = 3 * half // 2
    qkv_first = at.gather(qkv_half[:, :cut])
    hidden_other = at.to_core(hidden_in)

    vectors = (ln1_gain, ln1_bias, qv_bias, dense_bias, ln2_gain, ln2_bias, up_bias, down_bias)
    packed = jnp.concatenate(vectors)
    size = packed.shape[0]
    packed = jnp.pad(packed, (0, 16 * cut - size)).reshape(16, cut)
    qkv_second = at.gather(jnp.concatenate([qkv_half[:, cut:], packed]))
    qkv_pieces = qkv_first + qkv_second
    lines = -(-size // cut)
    held = jnp.stack([v[:, rd : rd + lines].reshape(nz, -1)[:, :size] for v in qkv_second])
    held = jnp.stack([lax.dynamic_index_in_dim(held, (at.x - x) % nx, 0, keepdims=False) for x in range(nx)], axis=1)
    packed = held.reshape(n, size).astype(F32)
    whole, start = [], 0
    for v in vectors:
        whole.append(packed[:, start : start + v.shape[0]].reshape(1, -1))
        start += v.shape[0]
    gain1, bias1, qv_b, dense_b, gain2, bias2, up_b, down_b = whole
    qv_half = lax.dynamic_index_in_dim(qv_b.reshape(2, 2, half), core, 1, keepdims=False)
    qkv_bias = jnp.concatenate([qv_half[:1], jnp.zeros((1, half), F32), qv_half[1:]], axis=1)
    up_b4 = lax.dynamic_index_in_dim(up_b.reshape(n, 2, 2, quarter), core, 1, keepdims=False)
    up_halves = jnp.concatenate(pick(up_b4[:, 0].reshape(1, -1), up_b4[:, 1].reshape(1, -1), y), axis=1)

    up_quarter = w_up.reshape(rd, n, 4, quarter)
    up_quarter = lax.dynamic_index_in_dim(up_quarter, core * 2 + y, 2, keepdims=False).reshape(rd, fq)
    up_first = at.gather(up_quarter[:, : fq // 2], True)
    dense_held = at.gather(lax.dynamic_slice_in_dim(w_dense, core * half, half, 1))
    give = jnp.stack([lax.dynamic_slice_in_dim(v, (1 - core) * (nz // 2), nz // 2, 0) for v in dense_held])
    dense_in = dense_held + [at.to_core(give)]
    up_second = at.gather(up_quarter[:, fq // 2 :], True)
    split = width * 5 // 8
    down_half = lax.dynamic_slice_in_dim(w_down, core * 2 * quarter, 2 * quarter, 0)
    down_quarter = lax.dynamic_slice_in_dim(down_half, y * quarter, quarter, 0)
    down_pieces = at.gather(down_quarter[:, :split], True)
    up_pieces = [v for i in range(2) for p in (up_first, up_second) for v in p[i * nx : (i + 1) * nx]]
    down_pieces = down_pieces + at.gather(down_half[:, split:])
    cot_other = at.to_core(cotangent)

    mac = 2 * 2 * rows * width
    nin, qkv, ctx, probs = call(
        functools.partial(attention_kernel, 2 * nx, rd),
        [((2 * rows, width), BF), ((2 * rows, 3 * half), BF), ((2 * rows, half), BF), ((2 * heads, rows, rows), BF)],
        [info, slopes, after(hidden_in, up_first[:1]), hidden_other, gain1, bias1, qkv_bias] + qkv_pieces,
        "ss" + "v" * 5 + "a" * 2 * nx,
        [pltpu.VMEM((width, 3 * half), BF), dma((2 * n,))],
        mac * 4 * half,
        "attn",
    )
    (part,) = call(
        functools.partial(dense_kernel, nx, rd),
        [((2 * rows, width), F32)],
        [info, after(ctx, up_second[:1])] + dense_in,
        "sv" + "a" * (nx + 1),
        [pltpu.VMEM((half, width), BF), dma((n,))],
        mac * half,
        "dense",
    )
    residual, mid = call(
        middle_kernel,
        [((2 * rows, width), F32), ((2 * rows, width), BF)],
        [after(hidden_in, up_second[1:nx] + down_pieces[:1]), hidden_other, part, at.to_core(part), dense_b, gain2, bias2],
        "v" * 7,
        name="middle",
    )
    act, slope = call(
        functools.partial(up_kernel, 4 * nx, rd),
        [((2 * rows, 2 * fq), BF), ((2 * rows, 2 * fq), F32)],
        [info, mid, up_halves] + up_pieces,
        "svv" + "a" * 4 * nx,
        [pltpu.VMEM((width, 2 * fq), BF), dma((4 * n,))],
        mac * 2 * fq,
        "up",
    )

    def scatter_y(left, right, per, cols, by_y, name):
        cols //= 2
        terms = call(
            functools.partial(grad_y_kernel, 2, by_y),
            [((nz, nx * per, cols), BF)] * 4,
            [info, left] + right,
            "sv" + "v" * len(right),
            name=name,
        )
        return [(terms[2 * p + 1], at.to_y(terms[2 * p])) for p in range(2)]

    def fold_y(terms, name):
        nz_, rows_, cols = terms[0].shape
        out = call(
            functools.partial(fold_y_kernel, nx),
            [((nz, rows_ // nx, cols), BF)] * nx,
            [info] + list(terms),
            "svv",
            name=name + "_y",
        )
        return over_x(out)

    def over_x(parts):
        return [parts[0]] + [at.to_x(parts[kx], kx) for kx in range(1, nx)]

    def fold_x(ins, name):
        nz_, per, cols = ins[0].shape
        outs = [((nz, per, cols * len(ins) // nx), BF)]
        return call(functools.partial(fold_x_kernel, nx), outs, ins, "v" * len(ins), name=name + "_x")[0]

    def finish_z(ends, name):
        _, per, cols = ends[0].shape
        total = sum(v.shape[2] for v in ends)
        return call(total_kernel, [((per, total), BF)], ends, "v" * len(ends), name=name + "_z")[0]

    down_terms = scatter_y(act, [cotangent, cot_other], quarter, width, False, "gdown")

    gpre, gpre_sums, gmid = call(
        functools.partial(feed_back_kernel, 4 * nx, rd, quarter),
        [((2 * rows, 2 * fq), BF), ((1, 2 * fq), F32), ((2 * rows, width), F32)],
        [info, cotangent, cot_other, slope] + up_pieces + down_pieces,
        "svvv" + "a" * 7 * nx,
        [pltpu.VMEM((width, 2 * fq), BF), pltpu.VMEM((2 * fq, width), BF), dma((4 * n,)), dma((4 * n,))],
        mac * 4 * fq,
        "feed_back",
    )
    gmid_recv = at.to_core(gmid)
    up_terms = call(
        functools.partial(up_grad_kernel, nx),
        [((nz, nx * rd, fq // 2), BF)] * 2 + [((nz, rd, fq), BF)] * nx,
        [info, mid, gpre],
        "svv",
        name="gup",
    )
    up_first_x = over_x(up_terms[2:])
    up_second_y = (up_terms[1], at.to_y(up_terms[0]))

    grad_res, grad_res_b, sums2, dqkv, qv_sums = call(
        functools.partial(attention_back_kernel, nx, rd),
        [
            ((rows, width), F32),
            ((2 * rows, width), BF),
            ((3, width), F32),
            ((2 * rows, 3 * half), BF),
            ((2, half), F32),
        ],
        [info, gmid, gmid_recv, residual, cotangent, cot_other, gain2, qkv, probs] + dense_in,
        "s" + "v" * 8 + "a" * (nx + 1),
        [pltpu.VMEM((half, width), BF), pltpu.VMEM((2 * rows, half), BF), dma((n,))],
        mac * 3 * half,
        "attn_back",
    )
    qkv_terms = scatter_y(nin, [dqkv], rd, cut, True, "gqkv")
    last = [qkv_terms[0][0]]

    def order(value):
        last[:] = [value[0] if isinstance(value, (list, tuple)) else value]
        return value

    up_sum = order(fold_x(after(up_first_x, last), "gup"))
    end_up = at.swap_z(up_sum)
    down_x = order(fold_y(after(down_terms[0], last), "gdown"))
    down_x = down_x + order(fold_y(after(down_terms[1], last), "gdown"))

    keep, give = call(
        dense_grad_kernel,
        [((nz // 2, nx * rd, half), BF)] * 2,
        [info, after(ctx, last), grad_res_b],
        "svv",
        name="gdense",
    )
    order(keep)
    up2_x = order(fold_y(after(up_second_y, last), "gup2"))
    parts = call(
        functools.partial(dense_place_kernel, nx),
        [((nz, rd, half), BF)] * nx,
        [info, after(keep, last), at.to_core(give)],
        "svv",
        name="gdense_c",
    )
    order(parts)
    dense_x = over_x(parts)
    down_sum = order(fold_x(after(down_x, last), "gdown"))
    end_down = at.swap_z(after(down_sum, [end_up]))
    order(end_up)
    qkv_x = order(fold_y(after(qkv_terms[0], last), "gqkv"))
    qkv_x = qkv_x + order(fold_y(after(qkv_terms[1], last), "gqkv"))
    up2_sum = order(fold_x(after(up2_x, last), "gup2"))
    end_up2 = at.swap_z(after(up2_sum, [end_down]))
    out_own, out_other = order(
        call(
            functools.partial(output_kernel, 3 * nx, quarter),
            [((rows, width), F32), ((rows, width), F32)],
            [info, after(act, last)] + down_pieces,
            "sv" + "a" * 3 * nx,
            [pltpu.VMEM((2 * fq, width), BF), dma((4 * n,))],
            name="output",
        )
    )
    order(end_down)
    dense_sum = order(fold_x(after(dense_x, last), "gdense"))
    end_dense = at.swap_z(after(dense_sum, [end_up2]))
    qkv_sum = order(fold_x(after(qkv_x, last), "gqkv"))
    end_qkv = at.swap_z(after(qkv_sum, [end_dense]))
    order(end_up2)
    norm_own, norm_other = order(
        call(
            functools.partial(normed_kernel, 2 * nx, rd),
            [((rows, width), F32), ((rows, width), F32)],
            [info, after(dqkv, last)] + qkv_pieces,
            "sv" + "a" * 2 * nx,
            [pltpu.VMEM((width, 3 * half), BF), dma((2 * n,))],
            name="gnorm",
        )
    )
    down_own = order(finish_z([after(end_down, last)], "gdown"))
    down_other = at.to_y(down_own)
    order(end_dense)
    up_part = order(finish_z(after([end_up, end_up2], last), "gup"))
    up_recv = at.to_y(up_part)
    dense_part = finish_z([end_dense], "gdense")
    qkv_own = finish_z([end_qkv], "gqkv")
    qkv_other = at.to_y(qkv_own)
    dense_mine = dense_part.astype(F32) + at.to_y(dense_part).astype(F32)
    grad_dense = jnp.concatenate(pick(dense_mine, at.to_core(dense_mine), core), axis=1)

    output = (residual[:rows] + (out_own + at.to_core(out_other)) + down_b).astype(BF)

    input_grad, sums1 = call(
        input_kernel,
        [((rows, width), F32), ((2, width), F32)],
        [norm_own, at.to_core(norm_other), hidden_in, grad_res, gain1],
        "v" * 5,
        name="input_grad",
    )

    down_y = jnp.concatenate(pick(down_own, down_other, y), axis=0)
    grad_down = jnp.concatenate(pick(down_y, at.to_core(down_y), core), axis=0).astype(F32)
    up_total = up_part[:, :fq].astype(F32) + up_recv[:, :fq].astype(F32)
    up_both = [v.astype(F32) for v in pick(up_part[:, fq:], up_recv[:, fq:], y)]
    up_c = jnp.concatenate([up_total] + up_both, axis=1)
    up_c = up_c.reshape(rd, 2, 2, n // 2, quarter).transpose(0, 1, 3, 2, 4).reshape(rd, n, 1, 2 * quarter)
    grad_up = jnp.concatenate(pick(up_c, at.to_core(up_c), core), axis=2).reshape(rd, ff)
    qkv_c = jnp.concatenate(pick(qkv_own, qkv_other, y), axis=1).reshape(rd, 3, 1, half)
    grad_qkv = jnp.concatenate(pick(qkv_c, at.to_core(qkv_c), core), axis=2).reshape(rd, 3 * width).astype(F32)

    grad_down_bias = jnp.sum(cotangent.astype(F32), axis=0)
    up_y = jnp.stack([g.reshape(n, quarter) for g in pick(gpre_sums[0, :fq], gpre_sums[0, fq:], y)], axis=1)
    on_core = jnp.arange(2) == core
    up_bias_all = jnp.where(on_core[None, :, None, None], up_y[:, None], 0.0).reshape(-1)
    qv_all = jnp.where(on_core[None, :, None], qv_sums[:, None], 0.0).reshape(-1)
    feed = jnp.concatenate([sums2.reshape(-1), grad_down_bias, up_bias_all, sums1.reshape(-1), qv_all])
    feed = at.sum_all(feed[None, :])[0]

    def own(start, size):
        per = size // n
        return lax.dynamic_slice_in_dim(feed, start + at.shard * per, per)

    return (
        output,
        input_grad,
        own(4 * width + ff, width),
        own(5 * width + ff, width),
        grad_qkv,
        own(6 * width + ff, 2 * width),
        grad_dense,
        own(2 * width, width),
        own(0, width),
        own(width, width),
        grad_up,
        own(4 * width, ff),
        grad_down,
        own(3 * width, width),
    )


def solution(mesh):
    both, rows, vector = P(("rep", "shard"), None), P("shard", None), P("shard")
    weights = (vector, vector, rows, vector, rows, vector, vector, vector, rows, vector, rows, vector)
    return jax.shard_map(
        functools.partial(on_device, mesh.shape["rep"], mesh.shape["shard"]),
        mesh=mesh,
        in_specs=(both, both) + weights,
        out_specs=(both, both) + weights,
        check_vma=False,
    )
```

```python
import functools
import math

import jax
import jax.numpy as jnp
import numpy as np
from jax import lax
from jax.experimental import pallas as pl
from jax.experimental.pallas import tpu as pltpu
from jax.sharding import PartitionSpec as P

H = 16
BF = jnp.bfloat16
F32 = jnp.float32
AXES = ("rep", "shard")
gelu_coef = math.sqrt(2.0 / math.pi)
VMEM_LIMIT = 60 * 2**20
COST = {'attn': 1000, 'dense': 1000, 'middle': 1000, 'up': 1000, 'gdown': 13.2, 'feed_back': 1000, 'gup': 16.2, 'attn_back': 1000, 'gqkv': 15.3, 'gdense': 9.0, 'output': 25.2, 'gnorm': 21.6, 'gdense_c': 6.6, 'input_grad': 11.4, 'gup_y': 7.8, 'gup_x': 7.8, 'gdown_x': 7.8, 'gqkv_x': 7.8, 'gqkv_y': 7.8, 'gdense_x': 7.8, 'gup_z': 7.8, 'gdown_z': 7.8, 'gdense_z': 7.8, 'gqkv_z': 7.8}


class Place:
    def __init__(self, reps, shards):
        self.reps, self.shards = reps, shards
        self.nx = max(n for n in (1, 2, 4, 8) if shards % n == 0 and n * n <= shards)
        self.nz = shards // self.nx
        rep, shard = lax.axis_index("rep"), lax.axis_index("shard")
        self.shard, self.waits = shard, [[]]
        table = [
            [r // 2, r % 2, v // self.nx, v % self.nx] for r in range(reps) for v in range(shards)
        ]
        row = lax.dynamic_slice_in_dim(jnp.asarray(np.array(table, np.int32)), rep * shards + shard, 1, 0)
        self.info = row[0]
        self.y, self.core, self.x = self.info[0], self.info[1], self.info[3]

    def _send(self, value, move):
        pairs = []
        for rep in range(self.reps):
            for shard in range(self.shards):
                y, core, z, x = move(rep // 2, rep % 2, shard // self.nx, shard % self.nx)
                pairs.append((rep * self.shards + shard, (y * 2 + core) * self.shards + z * self.nx + x))
        return lax.ppermute(value, AXES, pairs)

    def to_core(self, value):
        return self._send(value, lambda y, core, z, x: (y, 1 - core, z, x))

    def to_y(self, value):
        return self._send(value, lambda y, core, z, x: (1 - y, core, z, x))

    def to_z(self, value, k):
        return self._send(value, lambda y, core, z, x: (y, core, (z + k) % self.nz, x))

    def to_x(self, value, k):
        return self._send(value, lambda y, core, z, x: (y, core, z, (x + k) % self.nx))

    def swap_z(self, value):
        along = [[z * self.nx + x for z in range(self.nz)] for x in range(self.nx)]
        return lax.all_to_all(value, "shard", 0, 0, axis_index_groups=along, tiled=True)

    def gather(self, block, over_y=False):
        block = jnp.broadcast_to(block[None], (self.nz,) + block.shape)
        held = self.swap_z(after(block, self.waits.pop(0)))
        out = [held] + [self.to_x(held, kx) for kx in range(1, self.nx)]
        for i, values in enumerate(([held], out[1:])):
            self.hold(i, values)
        if over_y:
            out = out + [self.to_y(v) for v in out]
        return out

    def hold(self, steps, values):
        while len(self.waits) <= steps + 2:
            self.waits.append([])
        self.waits[steps] += values

    def sum_all(self, value):
        value = value + self.to_core(value)
        value = value + self.to_y(value)
        value = sum([self.to_x(value, k) for k in range(1, self.nx)], value)
        return sum([self.to_z(value, k) for k in range(1, self.nz)], value)


def after(value, waits):
    return lax.optimization_barrier((value, list(waits)))[0] if waits else value


def vmem():
    return pl.BlockSpec(memory_space=pltpu.VMEM)


def call(body, outs, ins, kinds, scratch=(), flops=0, name=None):
    spec = {
        "v": vmem(),
        "a": pl.BlockSpec(memory_space=pl.ANY),
        "s": pl.BlockSpec(memory_space=pltpu.SMEM),
    }
    moved = sum(v.size * v.dtype.itemsize for v in ins) + sum(math.prod(s) * jnp.dtype(t).itemsize for s, t in outs)
    return pl.pallas_call(
        body,
        out_shape=[jax.ShapeDtypeStruct(s, t) for s, t in outs],
        in_specs=[spec[k] for k in kinds],
        out_specs=[vmem() for _ in outs],
        scratch_shapes=list(scratch),
        compiler_params=pltpu.CompilerParams(vmem_limit_bytes=VMEM_LIMIT),
        cost_estimate=pl.CostEstimate(flops=int(1153.5e6 * COST.get(name, 2.5)), bytes_accessed=10**6, transcendentals=0),
        name=name,
    )(*ins)


def dot(a, b):
    return jnp.dot(a, b, preferred_element_type=F32)


def dot_tn(a, b):
    return lax.dot_general(a, b, (((0,), (0,)), ((), ())), preferred_element_type=F32)


def dot_nt(a, b):
    return lax.dot_general(a, b, (((1,), (1,)), ((), ())), preferred_element_type=F32)


def layer_norm(values_in):
    centre = values_in - jnp.mean(values_in, axis=-1, keepdims=True)
    inv_std = lax.rsqrt(jnp.mean(centre * centre, axis=-1, keepdims=True) + 1e-05)
    return (centre * inv_std, inv_std)


def norm_back(grad_normed, normed, inv_std):
    return inv_std * (
        grad_normed
        - jnp.mean(grad_normed, axis=-1, keepdims=True)
        - normed * jnp.mean(grad_normed * normed, axis=-1, keepdims=True)
    )


def aligned(value, step):
    return pl.multiple_of(value, step) if step % 8 == 0 else value


class Load:
    def __init__(self, sem):
        self.sem, self.copies = sem, []

    def copy(self, source, target):
        self.copies.append(pltpu.make_async_copy(source, target, self.sem.at[len(self.copies)]))

    def start(self):
        for copy in self.copies:
            copy.start()

    def wait(self):
        for copy in self.copies:
            copy.wait()

    def blocks(self, info, held, rows, target, col, first=0, base=0):
        nx, nz, cols = len(held), held[0].shape[0], held[0].shape[2]
        for kx, ref in enumerate(held):
            x = lax.rem(info[3] - kx + nx, nx)
            for z in range(nz):
                at = aligned(base + (z * nx + x) * rows, rows)
                self.copy(ref.at[z, pl.ds(first, rows), :], target.at[pl.ds(at, rows), pl.ds(col, cols)])

    def qkv(self, info, pieces, rd, target):
        nx = len(pieces) // 2
        for i in range(2):
            self.blocks(info, pieces[i * nx : (i + 1) * nx], rd, target, i * pieces[0].shape[2])

    def dense(self, info, held, other, rd, target):
        nx, nz, cols = len(held), held[0].shape[0], held[0].shape[2]
        for kx, ref in enumerate(held):
            x = lax.rem(info[3] - kx + nx, nx)
            for j in range(nz // 2):
                rows = pl.ds(aligned((j * nx + x) * rd, rd), rd)
                for core, source in ((info[1], ref.at[info[1] * (nz // 2) + j]), (1 - info[1], other.at[kx, j])):
                    lanes = pl.ds(pl.multiple_of(core * cols, 128), cols)
                    self.copy(source, target.at[rows, lanes])

    def up(self, info, pieces, rd, target):
        nx = len(pieces) // 4
        for i in range(4):
            self.blocks(info, pieces[i * nx : (i + 1) * nx], rd, target, i * pieces[0].shape[2])

    def down(self, info, pieces, quarter, target):
        nx, half = len(pieces) // 3, target.shape[0] // 2
        self.blocks(info, pieces[:nx], quarter, target, 0)
        self.blocks(info, pieces[nx : 2 * nx], quarter, target, 0, base=half)
        for part in range(2):
            base = jnp.bitwise_xor(info[0], part) * half
            self.blocks(info, pieces[2 * nx :], quarter, target, pieces[0].shape[2], part * quarter, base)


def attention_kernel(n, rd, *refs):
    info, slopes, own, other, gain, bias, qv, *rest = refs
    pieces, (nin_ref, qkv_ref, ctx_ref, probs_ref, wq, sem) = rest[:n], rest[n:]
    load = Load(sem)
    load.qkv(info, pieces, rd, wq)
    load.start()
    rows, width = own.shape
    half = width // 2
    for i, ref in enumerate((own, other)):
        normed, _ = layer_norm(ref[...].astype(F32))
        nin_ref[i * rows : (i + 1) * rows, :] = (normed * gain[...] + bias[...]).astype(BF)
    load.wait()
    tile = 256

    @pl.loop(0, 3 * half // tile)
    def _(t):
        cols = pl.ds(pl.multiple_of(t * tile, tile), tile)
        qkv_ref[:, cols] = (dot(nin_ref[...], wq[:, cols]) + qv[:, cols]).astype(BF)

    hd = width // H
    lane = lax.broadcasted_iota(jnp.int32, (rows, 2 * hd), 1)
    first = lane < hd
    q_pos = lax.broadcasted_iota(jnp.int32, (rows, rows), 0)
    k_pos = lax.broadcasted_iota(jnp.int32, (rows, rows), 1)
    distance = (k_pos - q_pos).astype(F32)
    seen = k_pos <= q_pos
    pairs = half // (2 * hd)

    @pl.loop(0, 2 * pairs, unroll=2)
    def _(step):
        seq, pair = step // pairs, step % pairs
        at = pl.ds(pl.multiple_of(seq * rows, rows), rows)
        lanes = [pl.ds(pl.multiple_of(part * half + pair * 2 * hd, 2 * hd), 2 * hd) for part in range(3)]
        q, k, v = (qkv_ref[at, where] for where in lanes)
        out = []
        for i in range(2):
            mine = first if i == 0 else jnp.logical_not(first)
            scores = dot_nt(jnp.where(mine, q, jnp.zeros_like(q)), k) * hd ** (-0.5) + slopes[pair * 2 + i] * distance
            scores = jnp.where(seen, scores, -1e30)
            e = jnp.exp(scores - jnp.max(scores, axis=-1, keepdims=True))
            probs = (e * (1.0 / jnp.sum(e, axis=-1, keepdims=True))).astype(BF)
            probs_ref[step * 2 + i] = probs
            out.append(dot(probs, v))
        ctx_ref[at, lanes[0]] = jnp.where(first, out[0], out[1]).astype(BF)


def dense_kernel(n, rd, *refs):
    info, ctx, *rest = refs
    held, (other, out_ref, wd, sem) = rest[:n], rest[n:]
    load = Load(sem)
    load.dense(info, held, other, rd, wd)
    load.start()
    load.wait()
    out_ref[...] = dot(ctx[...], wd[...])


def middle_kernel(own, other, part, recv, dense_b, gain, bias, res_ref, mid_ref):
    rows = own.shape[0]
    for i, ref in enumerate((own, other)):
        here, there = slice(i * rows, (i + 1) * rows), slice((1 - i) * rows, (2 - i) * rows)
        residual = ref[...].astype(F32) + (part[here, :] + recv[there, :]) + dense_b[...]
        res_ref[here, :] = residual
        normed, _ = layer_norm(residual)
        mid_ref[here, :] = (normed * gain[...] + bias[...]).astype(BF)


def up_kernel(n, rd, *refs):
    info, mid, up_b, *rest = refs
    pieces, (act_ref, slope_ref, wu, sem) = rest[:n], rest[n:]
    load = Load(sem)
    load.up(info, pieces, rd, wu)
    load.start()
    cols = wu.shape[1] // 2
    load.wait()
    tile = 256

    @pl.loop(0, 2 * cols // tile)
    def _(t):
        at = pl.ds(pl.multiple_of(t * tile, tile), tile)
        u = dot(mid[...], wu[:, at]) + up_b[:, at]
        square = u * u
        t_ = jnp.tanh(u * (gelu_coef + gelu_coef * 0.044715 * square))
        gate = 0.5 + 0.5 * t_
        value = u * gate
        act_ref[:, at] = value.astype(BF)
        slope_ref[:, at] = gate + value * (1.0 - t_) * (gelu_coef + 3.0 * 0.044715 * gelu_coef * square)


def feed_back_kernel(n, rd, quarter, *refs):
    info, own, other, slope, *rest = refs
    up_pieces, down_pieces, (gp_ref, gb_ref, gmid_ref, wu, wo, sem, sem2) = rest[:n], rest[n : n + n // 4 * 3], rest[n + n // 4 * 3 :]
    load, load2 = Load(sem), Load(sem2)
    load.down(info, down_pieces, quarter, wo)
    load2.up(info, up_pieces, rd, wu)
    load.start()
    load2.start()
    load.wait()
    cols = wu.shape[1] // 2
    rows = own.shape[0]
    tile = 256

    @pl.loop(0, 2 * cols // tile)
    def _(t):
        at = pl.ds(pl.multiple_of(t * tile, tile), tile)
        total = jnp.zeros((1, tile), F32)
        for i, ref in enumerate((own, other)):
            here = slice(i * rows, (i + 1) * rows)
            grad_pre = dot_nt(ref[...], wo[at, :]) * slope[here, at]
            gp_ref[here, at] = grad_pre.astype(BF)
            total = total + jnp.sum(grad_pre, axis=0, keepdims=True)
        gb_ref[:, at] = total

    width = own.shape[1]
    load2.wait()

    @pl.loop(0, width // tile)
    def _(t):
        at = pl.ds(pl.multiple_of(t * tile, tile), tile)
        gmid_ref[:, at] = dot_nt(gp_ref[...], wu[at, :])


def output_kernel(n, quarter, *refs):
    info, act, *rest = refs
    pieces, (own_ref, other_ref, wo, sem) = rest[:n], rest[n:]
    load = Load(sem)
    load.down(info, pieces, quarter, wo)
    load.start()
    load.wait()
    rows, width = own_ref.shape
    tile = 256

    @pl.loop(0, width // tile)
    def _(t):
        at = pl.ds(pl.multiple_of(t * tile, tile), tile)
        both = dot(act[...], wo[:, at])
        own_ref[:, at] = both[:rows]
        other_ref[:, at] = both[rows:]


def grad_y_kernel(parts, by_y, info, left, *refs):
    right, outs = refs[: -2 * parts], refs[-2 * parts :]
    tokens = right[0].shape[0]
    nz, rows, cols = outs[0].shape
    for which in range(2):
        for p in range(parts):
            out = outs[2 * p + which]
            for z in range(nz):
                total = None
                for i, ref in enumerate(right):
                    here = slice(i * tokens, (i + 1) * tokens)
                    first, start = z * rows, p * cols
                    if by_y:
                        y = info[0] if which == 1 else 1 - info[0]
                        start = pl.multiple_of((y * parts + p) * cols, 128)
                    else:
                        first += (1 - which) * nz * rows
                    term = dot_tn(left[here, first : first + rows], ref[:, pl.ds(start, cols)])
                    total = term if total is None else total + term
                out[z] = total.astype(BF)


def at_x(info, kx, nx, per, value):
    x = lax.rem(info[3] + kx, nx)
    picked = value[:per]
    for v in range(1, nx):
        picked = jnp.where(x == v, value[v * per : (v + 1) * per], picked)
    return picked


def up_grad_kernel(parts, nx, left, right, *outs):
    nz, rows, cols = outs[0].shape
    for p in range(parts):
        for z in range(nz):
            lhs = left[:, z * rows : (z + 1) * rows]
            for h in range(2):
                start = (h * parts + p) * cols
                outs[2 * p + 1 - h][z] = dot_tn(lhs, right[:, start : start + cols]).astype(BF)


def down_grad_kernel(p, nx, info, left, own, other, *outs):
    nz, per, cols = outs[0].shape
    per //= 2
    tokens = own.shape[0]
    half = left.shape[1] // 2
    here = slice(p * cols, (p + 1) * cols)
    for z in range(nz):
        for h in range(2):
            lanes = slice(h * half + z * nx * per, h * half + (z + 1) * nx * per)
            value = dot_tn(left[:tokens, lanes], own[:, here]) + dot_tn(left[tokens:, lanes], other[:, here])
            rows = pl.ds(aligned(jnp.bitwise_xor(info[0], h) * per, per), per)
            for kx in range(nx):
                outs[kx][z, rows, :] = at_x(info, kx, nx, per, value).astype(BF)


def fold_y_kernel(nx, info, mine, recv, *outs):
    per = outs[0].shape[1]
    for kx in range(nx):
        x = lax.rem(info[3] + kx, nx)
        at = pl.ds(aligned(x * per, per), per)
        outs[kx][...] = (mine[:, at, :].astype(F32) + recv[:, at, :].astype(F32)).astype(BF)


def dense_grad_kernel(info, left, right, keep, give):
    nz, rows, cols = keep.shape
    for z in range(nz):
        lhs = left[:, z * rows : (z + 1) * rows]
        for out, core in ((keep, info[1]), (give, 1 - info[1])):
            out[z] = dot_tn(lhs, right[:, pl.ds(pl.multiple_of(core * cols, 128), cols)]).astype(BF)


def dense_place_kernel(nx, info, mine, recv, *outs):
    nz, per = outs[0].shape[:2]
    for kx in range(nx):
        x = lax.rem(info[3] + kx, nx)
        at = pl.ds(aligned(x * per, per), per)
        outs[kx][pl.ds(info[1] * (nz // 2), nz // 2)] = mine[:, at, :]
        outs[kx][pl.ds((1 - info[1]) * (nz // 2), nz // 2)] = recv[:, at, :]


def total_kernel(*refs):
    out = refs[-1]
    at = 0
    for ref in refs[:-1]:
        cols = ref.shape[2]
        total = ref[0].astype(F32)
        for z in range(1, ref.shape[0]):
            total = total + ref[z].astype(F32)
        out[:, at : at + cols] = total.astype(BF)
        at += cols


def fold_x_kernel(nx, *refs):
    out = refs[-1]
    cols = refs[0].shape[2]
    for p in range(len(refs) // nx):
        total = refs[p * nx][...].astype(F32)
        for kx in range(1, nx):
            total = total + refs[p * nx + kx][...].astype(F32)
        out[:, :, p * cols : (p + 1) * cols] = total.astype(BF)


def attention_back_kernel(n, rd, *refs):
    info, part, recv, residual, own, other, gain, qkv, probs, *rest = refs
    held, outs = rest[:n], rest[n:]
    other_half, res_ref, resb_ref, sums_ref, dqkv_ref, qvb_ref, wd, gctx, sem = outs
    load = Load(sem)
    load.dense(info, held, other_half, rd, wd)
    load.start()
    rows, width = own.shape
    half = width // 2
    hd = width // H
    for i, ref in enumerate((own, other)):
        here, there = slice(i * rows, (i + 1) * rows), slice((1 - i) * rows, (2 - i) * rows)
        grad_mid = part[here, :] + recv[there, :]
        normed, inv_std = layer_norm(residual[here, :])
        grad_res = ref[...].astype(F32) + norm_back(grad_mid * gain[...], normed, inv_std)
        resb_ref[here, :] = grad_res.astype(BF)
        if i == 0:
            res_ref[...] = grad_res
            sums_ref[0:1, :] = jnp.sum(grad_mid * normed, axis=0, keepdims=True)
            sums_ref[1:2, :] = jnp.sum(grad_mid, axis=0, keepdims=True)
            sums_ref[2:3, :] = jnp.sum(grad_res, axis=0, keepdims=True)
    load.wait()
    gctx[...] = dot_nt(resb_ref[...], wd[...]).astype(BF)

    lane = lax.broadcasted_iota(jnp.int32, (rows, 2 * hd), 1)
    first = lane < hd
    pairs = half // (2 * hd)
    qvb_ref[...] = jnp.zeros_like(qvb_ref)

    @pl.loop(0, 2 * pairs, unroll=2)
    def _(step):
        seq, pair = step // pairs, step % pairs
        at = pl.ds(pl.multiple_of(seq * rows, rows), rows)
        lanes = [pl.ds(pl.multiple_of(p * half + pair * 2 * hd, 2 * hd), 2 * hd) for p in range(3)]
        q, k, v = (qkv[at, where] for where in lanes)
        g = gctx[at, lanes[0]]
        dq, dk, dv = 0.0, 0.0, 0.0
        for i in range(2):
            mine = first if i == 0 else jnp.logical_not(first)
            g_i = jnp.where(mine, g, jnp.zeros_like(g))
            prob = probs[step * 2 + i]
            prob_f = prob.astype(F32)
            grad_probs = dot_nt(g_i, v)
            delta = jnp.sum(prob_f * grad_probs, axis=-1, keepdims=True)
            grad_scores = (prob_f * (grad_probs - delta) * hd ** (-0.5)).astype(BF)
            dq = dq + dot(grad_scores, jnp.where(mine, k, jnp.zeros_like(k)))
            dk = dk + dot_tn(grad_scores, jnp.where(mine, q, jnp.zeros_like(q)))
            dv = dv + dot_tn(prob, g_i)
        for where, value in zip(lanes, (dq, dk, dv)):
            dqkv_ref[at, where] = value.astype(BF)
        for row, value in ((0, dq), (1, dv)):
            qvb_ref[row : row + 1, lanes[0]] = qvb_ref[row : row + 1, lanes[0]] + jnp.sum(value, axis=0, keepdims=True)


def normed_kernel(n, rd, *refs):
    info, dqkv, *rest = refs
    pieces, (own_ref, other_ref, wq, sem) = rest[:n], rest[n:]
    load = Load(sem)
    load.qkv(info, pieces, rd, wq)
    load.start()
    load.wait()
    rows, width = own_ref.shape
    tile = 256

    @pl.loop(0, width // tile)
    def _(t):
        at = pl.ds(pl.multiple_of(t * tile, tile), tile)
        both = dot_nt(dqkv[...], wq[at, :])
        own_ref[:, at] = both[:rows]
        other_ref[:, at] = both[rows:]


def input_kernel(own, recv, hidden, grad_res, gain, in_ref, sums_ref):
    grad_normed = own[...] + recv[...]
    normed, inv_std = layer_norm(hidden[...].astype(F32))
    sums_ref[0:1, :] = jnp.sum(grad_normed * normed, axis=0, keepdims=True)
    sums_ref[1:2, :] = jnp.sum(grad_normed, axis=0, keepdims=True)
    in_ref[...] = grad_res[...] + norm_back(grad_normed * gain[...], normed, inv_std)


def pick(pair_first, pair_second, index):
    flip = index == 1
    return jnp.where(flip, pair_second, pair_first), jnp.where(flip, pair_first, pair_second)


def on_device(
    reps,
    shards,
    hidden_in,
    cotangent,
    ln1_gain,
    ln1_bias,
    w_qkv,
    qv_bias,
    w_dense,
    dense_bias,
    ln2_gain,
    ln2_bias,
    w_up,
    up_bias,
    w_down,
    down_bias,
):
    at = Place(reps, shards)
    info, core, y = at.info, at.core, at.y
    nz, nx, n = at.nz, at.nx, shards
    rows, width = hidden_in.shape
    rd = w_qkv.shape[0]
    ff = w_up.shape[1]
    quarter = ff // shards // 4
    half = width // 2
    heads = H // 2
    hd = width // H
    fq = shards * quarter
    dma = pltpu.SemaphoreType.DMA
    slopes = jnp.asarray(2.0 ** (-8.0 * (np.arange(H) + 1.0) / H), F32)
    slopes = lax.dynamic_slice_in_dim(slopes, core * heads, heads)

    qkv_half = lax.dynamic_index_in_dim(w_qkv.reshape(rd, 3, 2, half), core, 2, keepdims=False)
    qkv_half = qkv_half.reshape(rd, 3 * half)
    cut = 3 * half // 2
    qkv_first = at.gather(qkv_half[:, :cut])
    hidden_other = at.to_core(hidden_in)

    vectors = (ln1_gain, ln1_bias, qv_bias, dense_bias, ln2_gain, ln2_bias, up_bias, down_bias)
    packed = jnp.concatenate(vectors)
    size = packed.shape[0]
    packed = jnp.pad(packed, (0, 16 * cut - size)).reshape(16, cut)
    qkv_second = at.gather(jnp.concatenate([qkv_half[:, cut:], packed]))
    qkv_pieces = qkv_first + qkv_second
    lines = -(-size // cut)
    held = jnp.stack([v[:, rd : rd + lines].reshape(nz, -1)[:, :size] for v in qkv_second])
    held = jnp.stack([lax.dynamic_index_in_dim(held, (at.x - x) % nx, 0, keepdims=False) for x in range(nx)], axis=1)
    packed = held.reshape(n, size).astype(F32)
    whole, start = [], 0
    for v in vectors:
        whole.append(packed[:, start : start + v.shape[0]].reshape(1, -1))
        start += v.shape[0]
    gain1, bias1, qv_b, dense_b, gain2, bias2, up_b, down_b = whole
    qv_half = lax.dynamic_index_in_dim(qv_b.reshape(2, 2, half), core, 1, keepdims=False)
    qkv_bias = jnp.concatenate([qv_half[:1], jnp.zeros((1, half), F32), qv_half[1:]], axis=1)
    up_b4 = lax.dynamic_index_in_dim(up_b.reshape(n, 2, 2, quarter), core, 1, keepdims=False)
    up_halves = jnp.concatenate(pick(up_b4[:, 0].reshape(1, -1), up_b4[:, 1].reshape(1, -1), y), axis=1)

    up_quarter = w_up.reshape(rd, n, 4, quarter)
    up_quarter = lax.dynamic_index_in_dim(up_quarter, core * 2 + y, 2, keepdims=False).reshape(rd, fq)
    up_first = at.gather(up_quarter[:, : fq // 2], True)
    dense_held = at.gather(lax.dynamic_slice_in_dim(w_dense, core * half, half, 1))
    give = jnp.stack([lax.dynamic_slice_in_dim(v, (1 - core) * (nz // 2), nz // 2, 0) for v in dense_held])
    dense_in = dense_held + [at.to_core(give)]
    up_second = at.gather(up_quarter[:, fq // 2 :], True)
    split = width * 5 // 8
    down_half = lax.dynamic_slice_in_dim(w_down, core * 2 * quarter, 2 * quarter, 0)
    down_quarter = lax.dynamic_slice_in_dim(down_half, y * quarter, quarter, 0)
    down_pieces = at.gather(down_quarter[:, :split], True)
    up_pieces = [v for i in range(2) for p in (up_first, up_second) for v in p[i * nx : (i + 1) * nx]]
    down_pieces = down_pieces + at.gather(down_half[:, split:])
    cot_other = at.to_core(cotangent)

    mac = 2 * 2 * rows * width
    nin, qkv, ctx, probs = call(
        functools.partial(attention_kernel, 2 * nx, rd),
        [((2 * rows, width), BF), ((2 * rows, 3 * half), BF), ((2 * rows, half), BF), ((2 * heads, rows, rows), BF)],
        [info, slopes, after(hidden_in, up_first[:1]), hidden_other, gain1, bias1, qkv_bias] + qkv_pieces,
        "ss" + "v" * 5 + "a" * 2 * nx,
        [pltpu.VMEM((width, 3 * half), BF), dma((2 * n,))],
        mac * 4 * half,
        "attn",
    )
    (part,) = call(
        functools.partial(dense_kernel, nx, rd),
        [((2 * rows, width), F32)],
        [info, after(ctx, up_second[:1])] + dense_in,
        "sv" + "a" * (nx + 1),
        [pltpu.VMEM((half, width), BF), dma((n,))],
        mac * half,
        "dense",
    )
    residual, mid = call(
        middle_kernel,
        [((2 * rows, width), F32), ((2 * rows, width), BF)],
        [after(hidden_in, up_second[1:nx] + down_pieces[:1]), hidden_other, part, at.to_core(part), dense_b, gain2, bias2],
        "v" * 7,
        name="middle",
    )
    act, slope = call(
        functools.partial(up_kernel, 4 * nx, rd),
        [((2 * rows, 2 * fq), BF), ((2 * rows, 2 * fq), F32)],
        [info, mid, up_halves] + up_pieces,
        "svv" + "a" * 4 * nx,
        [pltpu.VMEM((width, 2 * fq), BF), dma((4 * n,))],
        mac * 2 * fq,
        "up",
    )

    def scatter_y(left, right, per, cols, by_y, name):
        cols //= 2
        terms = call(
            functools.partial(grad_y_kernel, 2, by_y),
            [((nz, nx * per, cols), BF)] * 4,
            [info, left] + right,
            "sv" + "v" * len(right),
            name=name,
        )
        return [(terms[2 * p + 1], at.to_y(terms[2 * p])) for p in range(2)]

    def fold_y(terms, name):
        nz_, rows_, cols = terms[0].shape
        out = call(
            functools.partial(fold_y_kernel, nx),
            [((nz, rows_ // nx, cols), BF)] * nx,
            [info] + list(terms),
            "svv",
            name=name + "_y",
        )
        return over_x(out)

    def over_x(parts):
        return [parts[0]] + [at.to_x(parts[kx], kx) for kx in range(1, nx)]

    def fold_x(ins, name):
        nz_, per, cols = ins[0].shape
        outs = [((nz, per, cols * len(ins) // nx), BF)]
        return call(functools.partial(fold_x_kernel, nx), outs, ins, "v" * len(ins), name=name + "_x")[0]

    def finish_z(ends, name):
        _, per, cols = ends[0].shape
        total = sum(v.shape[2] for v in ends)
        return call(total_kernel, [((per, total), BF)], ends, "v" * len(ends), name=name + "_z")[0]

    down_x, before = [], []
    for p in range(2):
        down_terms = call(
            functools.partial(down_grad_kernel, p, nx),
            [((nz, 2 * quarter, width // 2), BF)] * nx,
            [info, after(act, before), cotangent, cot_other],
            "svvv",
            name="gdown",
        )
        before = [down_terms[0]]
        down_x.append(over_x(down_terms))

    gpre, gpre_sums, gmid = call(
        functools.partial(feed_back_kernel, 4 * nx, rd, quarter),
        [((2 * rows, 2 * fq), BF), ((1, 2 * fq), F32), ((2 * rows, width), F32)],
        [info, cotangent, cot_other, slope] + up_pieces + down_pieces,
        "svvv" + "a" * 7 * nx,
        [pltpu.VMEM((width, 2 * fq), BF), pltpu.VMEM((2 * fq, width), BF), dma((4 * n,)), dma((4 * n,))],
        mac * 4 * fq,
        "feed_back",
    )
    gmid_recv = at.to_core(gmid)
    up_terms = call(
        functools.partial(up_grad_kernel, 2, nx),
        [((nz, nx * rd, fq // 2), BF)] * 4,
        [mid, gpre],
        "vv",
        name="gup",
    )
    up_y = [(up_terms[2 * p + 1], at.to_y(up_terms[2 * p])) for p in range(2)]
    down_sum = fold_x(after(down_x[0], [up_terms[0]]), "gdown")
    end_down = [at.swap_z(down_sum)]

    grad_res, grad_res_b, sums2, dqkv, qv_sums = call(
        functools.partial(attention_back_kernel, nx, rd),
        [
            ((rows, width), F32),
            ((2 * rows, width), BF),
            ((3, width), F32),
            ((2 * rows, 3 * half), BF),
            ((2, half), F32),
        ],
        [info, after(gmid, [down_sum]), gmid_recv, residual, cotangent, cot_other, gain2, qkv, probs] + dense_in,
        "s" + "v" * 8 + "a" * (nx + 1),
        [pltpu.VMEM((half, width), BF), pltpu.VMEM((2 * rows, half), BF), dma((n,))],
        mac * 3 * half,
        "attn_back",
    )
    qkv_terms = scatter_y(nin, [dqkv], rd, cut, True, "gqkv")
    last = [qkv_terms[0][0]]

    def order(value):
        last[:] = [value[0] if isinstance(value, (list, tuple)) else value]
        return value

    down_sum2 = order(fold_x(after(down_x[1], last), "gdown"))
    end_down.append(at.swap_z(after(down_sum2, end_down)))
    up_x = order(fold_y(after(up_y[0], last), "gup"))
    keep, give = call(
        dense_grad_kernel,
        [((nz // 2, nx * rd, half), BF)] * 2,
        [info, after(ctx, last), grad_res_b],
        "svv",
        name="gdense",
    )
    order(keep)
    out_own, out_other = order(
        call(
            functools.partial(output_kernel, 3 * nx, quarter),
            [((rows, width), F32), ((rows, width), F32)],
            [info, after(act, last)] + down_pieces,
            "sv" + "a" * 3 * nx,
            [pltpu.VMEM((2 * fq, width), BF), dma((4 * n,))],
            name="output",
        )
    )
    up_x = up_x + order(fold_y(after(up_y[1], last), "gup"))
    parts = call(
        functools.partial(dense_place_kernel, nx),
        [((nz, rd, half), BF)] * nx,
        [info, after(keep, last), at.to_core(give)],
        "svv",
        name="gdense_c",
    )
    order(parts)
    dense_x = over_x(parts)
    up_sum = order(fold_x(after(up_x, last), "gup"))
    end_up = at.swap_z(after(up_sum, end_down[1:]))
    order(end_down[1])
    qkv_x = order(fold_y(after(qkv_terms[0], last), "gqkv"))
    qkv_x = qkv_x + order(fold_y(after(qkv_terms[1], last), "gqkv"))
    order(end_up)
    norm_own, norm_other = order(
        call(
            functools.partial(normed_kernel, 2 * nx, rd),
            [((rows, width), F32), ((rows, width), F32)],
            [info, after(dqkv, last)] + qkv_pieces,
            "sv" + "a" * 2 * nx,
            [pltpu.VMEM((width, 3 * half), BF), dma((2 * n,))],
            name="gnorm",
        )
    )
    qkv_sum = order(fold_x(after(qkv_x, last), "gqkv"))
    end_qkv = at.swap_z(after(qkv_sum, [end_up]))
    order(end_up)
    down_part = order(finish_z(after(end_down, last), "gdown"))
    down_recv = at.to_y(down_part)
    dense_sum = order(fold_x(after(dense_x, last), "gdense"))
    end_dense = at.swap_z(after(dense_sum, [end_qkv]))
    up_own = order(finish_z([after(end_up, last)], "gup"))
    up_other = at.to_y(up_own)
    order(end_qkv)
    qkv_own = order(finish_z([after(end_qkv, last)], "gqkv"))
    qkv_other = at.to_y(qkv_own)
    dense_part = order(finish_z([after(end_dense, last)], "gdense"))
    dense_mine = dense_part.astype(F32) + at.to_y(dense_part).astype(F32)
    grad_dense = jnp.concatenate(pick(dense_mine, at.to_core(dense_mine), core), axis=1)

    output = (residual[:rows] + (after(out_own, [dense_part]) + at.to_core(out_other)) + down_b).astype(BF)

    input_grad, sums1 = call(
        input_kernel,
        [((rows, width), F32), ((2, width), F32)],
        [norm_own, at.to_core(norm_other), hidden_in, grad_res, gain1],
        "v" * 5,
        name="input_grad",
    )

    down_c = down_part.astype(F32) + down_recv.astype(F32)
    grad_down = jnp.concatenate(pick(down_c, at.to_core(down_c), core), axis=0)
    up_c = jnp.stack([v.reshape(rd, n, quarter) for v in pick(up_own, up_other, y)], axis=2)
    grad_up = jnp.stack(pick(up_c, at.to_core(up_c), core), axis=2).reshape(rd, ff).astype(F32)
    qkv_c = jnp.concatenate(pick(qkv_own, qkv_other, y), axis=1).reshape(rd, 3, 1, half)
    grad_qkv = jnp.concatenate(pick(qkv_c, at.to_core(qkv_c), core), axis=2).reshape(rd, 3 * width).astype(F32)

    grad_down_bias = jnp.sum(cotangent.astype(F32), axis=0)
    up_y = jnp.stack([g.reshape(n, quarter) for g in pick(gpre_sums[0, :fq], gpre_sums[0, fq:], y)], axis=1)
    on_core = jnp.arange(2) == core
    up_bias_all = jnp.where(on_core[None, :, None, None], up_y[:, None], 0.0).reshape(-1)
    qv_all = jnp.where(on_core[None, :, None], qv_sums[:, None], 0.0).reshape(-1)
    feed = jnp.concatenate([sums2.reshape(-1), grad_down_bias, up_bias_all, sums1.reshape(-1), qv_all])
    feed = at.sum_all(feed[None, :])[0]

    def own(start, size):
        per = size // n
        return lax.dynamic_slice_in_dim(feed, start + at.shard * per, per)

    return (
        output,
        input_grad,
        own(4 * width + ff, width),
        own(5 * width + ff, width),
        grad_qkv,
        own(6 * width + ff, 2 * width),
        grad_dense,
        own(2 * width, width),
        own(0, width),
        own(width, width),
        grad_up,
        own(4 * width, ff),
        grad_down,
        own(3 * width, width),
    )


def solution(mesh):
    both, rows, vector = P(("rep", "shard"), None), P("shard", None), P("shard")
    weights = (vector, vector, rows, vector, rows, vector, vector, vector, rows, vector, rows, vector)
    return jax.shard_map(
        functools.partial(on_device, mesh.shape["rep"], mesh.shape["shard"]),
        mesh=mesh,
        in_specs=(both, both) + weights,
        out_specs=(both, both) + weights,
        check_vma=False,
    )
```

```python
import functools
import math

import jax
import jax.numpy as jnp
import numpy as np
from jax import lax
from jax.experimental import pallas as pl
from jax.experimental.pallas import tpu as pltpu
from jax.sharding import PartitionSpec as P

H = 16
BF = jnp.bfloat16
F32 = jnp.float32
AXES = ("rep", "shard")
gelu_coef = math.sqrt(2.0 / math.pi)
VMEM_LIMIT = 60 * 2**20
COST = {'attn': 1000, 'dense': 1000, 'middle': 1000, 'up': 1000, 'gdown': 13.2, 'feed_back': 1000, 'gup': 16.2, 'attn_back': 1000, 'gqkv': 15.3, 'gdense': 9.0, 'output': 25.2, 'gnorm': 21.6, 'gdense_c': 6.6, 'input_grad': 11.4, 'gup_y': 7.8, 'gup_x': 7.8, 'gdown_x': 7.8, 'gqkv_x': 7.8, 'gqkv_y': 7.8, 'gdense_x': 7.8, 'gup_z': 7.8, 'gdown_z': 7.8, 'gdense_z': 7.8, 'gqkv_z': 7.8}


class Place:
    def __init__(self, reps, shards):
        self.reps, self.shards = reps, shards
        self.nx = max(n for n in (1, 2, 4, 8) if shards % n == 0 and n * n <= shards)
        self.nz = shards // self.nx
        rep, shard = lax.axis_index("rep"), lax.axis_index("shard")
        self.shard, self.waits = shard, [[]]
        table = [
            [r // 2, r % 2, v // self.nx, v % self.nx] for r in range(reps) for v in range(shards)
        ]
        row = lax.dynamic_slice_in_dim(jnp.asarray(np.array(table, np.int32)), rep * shards + shard, 1, 0)
        self.info = row[0]
        self.y, self.core, self.x = self.info[0], self.info[1], self.info[3]

    def _send(self, value, move):
        pairs = []
        for rep in range(self.reps):
            for shard in range(self.shards):
                y, core, z, x = move(rep // 2, rep % 2, shard // self.nx, shard % self.nx)
                pairs.append((rep * self.shards + shard, (y * 2 + core) * self.shards + z * self.nx + x))
        return lax.ppermute(value, AXES, pairs)

    def to_core(self, value):
        return self._send(value, lambda y, core, z, x: (y, 1 - core, z, x))

    def to_y(self, value):
        return self._send(value, lambda y, core, z, x: (1 - y, core, z, x))

    def to_z(self, value, k):
        return self._send(value, lambda y, core, z, x: (y, core, (z + k) % self.nz, x))

    def to_x(self, value, k):
        return self._send(value, lambda y, core, z, x: (y, core, z, (x + k) % self.nx))

    def swap_z(self, value):
        along = [[z * self.nx + x for z in range(self.nz)] for x in range(self.nx)]
        return lax.all_to_all(value, "shard", 0, 0, axis_index_groups=along, tiled=True)

    def gather(self, block, over_y=False):
        block = jnp.broadcast_to(block[None], (self.nz,) + block.shape)
        held = self.swap_z(after(block, self.waits.pop(0)))
        out = [held] + [self.to_x(held, kx) for kx in range(1, self.nx)]
        for i, values in enumerate(([held], out[1:])):
            self.hold(i, values)
        if over_y:
            out = out + [self.to_y(v) for v in out]
        return out

    def hold(self, steps, values):
        while len(self.waits) <= steps + 2:
            self.waits.append([])
        self.waits[steps] += values

    def sum_all(self, value):
        value = value + self.to_core(value)
        value = value + self.to_y(value)
        value = sum([self.to_x(value, k) for k in range(1, self.nx)], value)
        return sum([self.to_z(value, k) for k in range(1, self.nz)], value)


def after(value, waits):
    return lax.optimization_barrier((value, list(waits)))[0] if waits else value


def vmem():
    return pl.BlockSpec(memory_space=pltpu.VMEM)


def call(body, outs, ins, kinds, scratch=(), flops=0, name=None):
    spec = {
        "v": vmem(),
        "a": pl.BlockSpec(memory_space=pl.ANY),
        "s": pl.BlockSpec(memory_space=pltpu.SMEM),
    }
    moved = sum(v.size * v.dtype.itemsize for v in ins) + sum(math.prod(s) * jnp.dtype(t).itemsize for s, t in outs)
    return pl.pallas_call(
        body,
        out_shape=[jax.ShapeDtypeStruct(s, t) for s, t in outs],
        in_specs=[spec[k] for k in kinds],
        out_specs=[vmem() for _ in outs],
        scratch_shapes=list(scratch),
        compiler_params=pltpu.CompilerParams(vmem_limit_bytes=VMEM_LIMIT),
        cost_estimate=pl.CostEstimate(flops=int(1153.5e6 * COST.get(name, 2.5)), bytes_accessed=10**6, transcendentals=0),
        name=name,
    )(*ins)


def dot(a, b):
    return jnp.dot(a, b, preferred_element_type=F32)


def dot_tn(a, b):
    return lax.dot_general(a, b, (((0,), (0,)), ((), ())), preferred_element_type=F32)


def dot_nt(a, b):
    return lax.dot_general(a, b, (((1,), (1,)), ((), ())), preferred_element_type=F32)


def layer_norm(values_in):
    centre = values_in - jnp.mean(values_in, axis=-1, keepdims=True)
    inv_std = lax.rsqrt(jnp.mean(centre * centre, axis=-1, keepdims=True) + 1e-05)
    return (centre * inv_std, inv_std)


def norm_back(grad_normed, normed, inv_std):
    return inv_std * (
        grad_normed
        - jnp.mean(grad_normed, axis=-1, keepdims=True)
        - normed * jnp.mean(grad_normed * normed, axis=-1, keepdims=True)
    )


def aligned(value, step):
    return pl.multiple_of(value, step) if step % 8 == 0 else value


class Load:
    def __init__(self, sem):
        self.sem, self.copies = sem, []

    def copy(self, source, target):
        self.copies.append(pltpu.make_async_copy(source, target, self.sem.at[len(self.copies)]))

    def start(self):
        for copy in self.copies:
            copy.start()

    def wait(self):
        for copy in self.copies:
            copy.wait()

    def blocks(self, info, held, rows, target, col, first=0, base=0):
        nx, nz, cols = len(held), held[0].shape[0], held[0].shape[2]
        for kx, ref in enumerate(held):
            x = lax.rem(info[3] - kx + nx, nx)
            for z in range(nz):
                at = aligned(base + (z * nx + x) * rows, rows)
                self.copy(ref.at[z, pl.ds(first, rows), :], target.at[pl.ds(at, rows), pl.ds(col, cols)])

    def qkv(self, info, pieces, rd, target):
        nx = len(pieces) // 2
        for i in range(2):
            self.blocks(info, pieces[i * nx : (i + 1) * nx], rd, target, i * pieces[0].shape[2])

    def dense(self, info, held, other, rd, target):
        nx, nz, cols = len(held), held[0].shape[0], held[0].shape[2]
        for kx, ref in enumerate(held):
            x = lax.rem(info[3] - kx + nx, nx)
            for j in range(nz // 2):
                rows = pl.ds(aligned((j * nx + x) * rd, rd), rd)
                for core, source in ((info[1], ref.at[info[1] * (nz // 2) + j]), (1 - info[1], other.at[kx, j])):
                    lanes = pl.ds(pl.multiple_of(core * cols, 128), cols)
                    self.copy(source, target.at[rows, lanes])

    def up(self, info, pieces, rd, target):
        nx = len(pieces) // 4
        for i in range(4):
            self.blocks(info, pieces[i * nx : (i + 1) * nx], rd, target, i * pieces[0].shape[2])

    def down(self, info, pieces, quarter, target):
        nx, half = len(pieces) // 3, target.shape[0] // 2
        self.blocks(info, pieces[:nx], quarter, target, 0)
        self.blocks(info, pieces[nx : 2 * nx], quarter, target, 0, base=half)
        for part in range(2):
            base = jnp.bitwise_xor(info[0], part) * half
            self.blocks(info, pieces[2 * nx :], quarter, target, pieces[0].shape[2], part * quarter, base)


def attention_kernel(n, rd, *refs):
    info, slopes, own, other, gain, bias, qv, *rest = refs
    pieces, (nin_ref, qkv_ref, ctx_ref, probs_ref, wq, sem) = rest[:n], rest[n:]
    load = Load(sem)
    load.qkv(info, pieces, rd, wq)
    load.start()
    rows, width = own.shape
    half = width // 2
    for i, ref in enumerate((own, other)):
        normed, _ = layer_norm(ref[...].astype(F32))
        nin_ref[i * rows : (i + 1) * rows, :] = (normed * gain[...] + bias[...]).astype(BF)
    load.wait()
    tile = 256

    @pl.loop(0, 3 * half // tile, unroll=4)
    def _(t):
        cols = pl.ds(pl.multiple_of(t * tile, tile), tile)
        qkv_ref[:, cols] = (dot(nin_ref[...], wq[:, cols]) + qv[:, cols]).astype(BF)

    hd = width // H
    lane = lax.broadcasted_iota(jnp.int32, (rows, 2 * hd), 1)
    first = lane < hd
    q_pos = lax.broadcasted_iota(jnp.int32, (rows, rows), 0)
    k_pos = lax.broadcasted_iota(jnp.int32, (rows, rows), 1)
    distance = (k_pos - q_pos).astype(F32)
    seen = k_pos <= q_pos
    pairs = half // (2 * hd)

    @pl.loop(0, 2 * pairs, unroll=8)
    def _(step):
        seq, pair = step // pairs, step % pairs
        at = pl.ds(pl.multiple_of(seq * rows, rows), rows)
        lanes = [pl.ds(pl.multiple_of(part * half + pair * 2 * hd, 2 * hd), 2 * hd) for part in range(3)]
        q, k, v = (qkv_ref[at, where] for where in lanes)
        out = []
        for i in range(2):
            mine = first if i == 0 else jnp.logical_not(first)
            scores = dot_nt(jnp.where(mine, q, jnp.zeros_like(q)), k) * hd ** (-0.5) + slopes[pair * 2 + i] * distance
            scores = jnp.where(seen, scores, -1e30)
            e = jnp.exp(scores - jnp.max(scores, axis=-1, keepdims=True))
            probs = (e * (1.0 / jnp.sum(e, axis=-1, keepdims=True))).astype(BF)
            probs_ref[step * 2 + i] = probs
            out.append(dot(probs, v))
        ctx_ref[at, lanes[0]] = jnp.where(first, out[0], out[1]).astype(BF)


def dense_kernel(n, rd, *refs):
    info, ctx, *rest = refs
    held, (other, out_ref, wd, sem) = rest[:n], rest[n:]
    load = Load(sem)
    load.dense(info, held, other, rd, wd)
    load.start()
    load.wait()
    out_ref[...] = dot(ctx[...], wd[...])


def middle_kernel(own, other, part, recv, dense_b, gain, bias, res_ref, mid_ref):
    rows = own.shape[0]
    for i, ref in enumerate((own, other)):
        here, there = slice(i * rows, (i + 1) * rows), slice((1 - i) * rows, (2 - i) * rows)
        residual = ref[...].astype(F32) + (part[here, :] + recv[there, :]) + dense_b[...]
        res_ref[here, :] = residual
        normed, _ = layer_norm(residual)
        mid_ref[here, :] = (normed * gain[...] + bias[...]).astype(BF)


def up_kernel(n, rd, *refs):
    info, mid, up_b, *rest = refs
    pieces, (act_ref, slope_ref, wu, sem) = rest[:n], rest[n:]
    load = Load(sem)
    load.up(info, pieces, rd, wu)
    load.start()
    cols = wu.shape[1] // 2
    load.wait()
    tile = 256

    @pl.loop(0, 2 * cols // tile, unroll=4)
    def _(t):
        at = pl.ds(pl.multiple_of(t * tile, tile), tile)
        u = dot(mid[...], wu[:, at]) + up_b[:, at]
        square = u * u
        t_ = jnp.tanh(u * (gelu_coef + gelu_coef * 0.044715 * square))
        gate = 0.5 + 0.5 * t_
        value = u * gate
        act_ref[:, at] = value.astype(BF)
        slope_ref[:, at] = gate + value * (1.0 - t_) * (gelu_coef + 3.0 * 0.044715 * gelu_coef * square)


def feed_back_kernel(n, rd, quarter, *refs):
    info, own, other, slope, *rest = refs
    up_pieces, down_pieces, (gp_ref, gb_ref, gmid_ref, wu, wo, sem, sem2) = rest[:n], rest[n : n + n // 4 * 3], rest[n + n // 4 * 3 :]
    load, load2 = Load(sem), Load(sem2)
    load.down(info, down_pieces, quarter, wo)
    load2.up(info, up_pieces, rd, wu)
    load.start()
    load2.start()
    load.wait()
    cols = wu.shape[1] // 2
    rows = own.shape[0]
    tile = 256

    @pl.loop(0, 2 * cols // tile, unroll=4)
    def _(t):
        at = pl.ds(pl.multiple_of(t * tile, tile), tile)
        total = jnp.zeros((1, tile), F32)
        for i, ref in enumerate((own, other)):
            here = slice(i * rows, (i + 1) * rows)
            grad_pre = dot_nt(ref[...], wo[at, :]) * slope[here, at]
            gp_ref[here, at] = grad_pre.astype(BF)
            total = total + jnp.sum(grad_pre, axis=0, keepdims=True)
        gb_ref[:, at] = total

    width = own.shape[1]
    load2.wait()

    @pl.loop(0, width // tile, unroll=4)
    def _(t):
        at = pl.ds(pl.multiple_of(t * tile, tile), tile)
        gmid_ref[:, at] = dot_nt(gp_ref[...], wu[at, :])


def output_kernel(n, quarter, *refs):
    info, act, *rest = refs
    pieces, (own_ref, other_ref, wo, sem) = rest[:n], rest[n:]
    load = Load(sem)
    load.down(info, pieces, quarter, wo)
    load.start()
    load.wait()
    rows, width = own_ref.shape
    tile = 256

    @pl.loop(0, width // tile, unroll=4)
    def _(t):
        at = pl.ds(pl.multiple_of(t * tile, tile), tile)
        both = dot(act[...], wo[:, at])
        own_ref[:, at] = both[:rows]
        other_ref[:, at] = both[rows:]


def grad_y_kernel(parts, by_y, info, left, *refs):
    right, outs = refs[: -2 * parts], refs[-2 * parts :]
    tokens = right[0].shape[0]
    nz, rows, cols = outs[0].shape
    for which in range(2):
        for p in range(parts):
            out = outs[2 * p + which]
            for z in range(nz):
                total = None
                for i, ref in enumerate(right):
                    here = slice(i * tokens, (i + 1) * tokens)
                    first, start = z * rows, p * cols
                    if by_y:
                        y = info[0] if which == 1 else 1 - info[0]
                        start = pl.multiple_of((y * parts + p) * cols, 128)
                    else:
                        first += (1 - which) * nz * rows
                    term = dot_tn(left[here, first : first + rows], ref[:, pl.ds(start, cols)])
                    total = term if total is None else total + term
                out[z] = total.astype(BF)


def at_x(info, kx, nx, per, value):
    x = lax.rem(info[3] + kx, nx)
    picked = value[:per]
    for v in range(1, nx):
        picked = jnp.where(x == v, value[v * per : (v + 1) * per], picked)
    return picked


def up_grad_kernel(parts, nx, left, right, *outs):
    nz, rows, cols = outs[0].shape
    for p in range(parts):
        for z in range(nz):
            lhs = left[:, z * rows : (z + 1) * rows]
            for h in range(2):
                start = (h * parts + p) * cols
                outs[2 * p + 1 - h][z] = dot_tn(lhs, right[:, start : start + cols]).astype(BF)


def down_grad_kernel(p, nx, info, left, own, other, *outs):
    nz, per, cols = outs[0].shape
    per //= 2
    tokens = own.shape[0]
    half = left.shape[1] // 2
    here = slice(p * cols, (p + 1) * cols)
    for z in range(nz):
        for h in range(2):
            lanes = slice(h * half + z * nx * per, h * half + (z + 1) * nx * per)
            value = dot_tn(left[:tokens, lanes], own[:, here]) + dot_tn(left[tokens:, lanes], other[:, here])
            rows = pl.ds(aligned(jnp.bitwise_xor(info[0], h) * per, per), per)
            for kx in range(nx):
                outs[kx][z, rows, :] = at_x(info, kx, nx, per, value).astype(BF)


def fold_y_kernel(nx, info, mine, recv, *outs):
    per = outs[0].shape[1]
    for kx in range(nx):
        x = lax.rem(info[3] + kx, nx)
        at = pl.ds(aligned(x * per, per), per)
        outs[kx][...] = (mine[:, at, :].astype(F32) + recv[:, at, :].astype(F32)).astype(BF)


def dense_grad_kernel(info, left, right, keep, give):
    nz, rows, cols = keep.shape
    for z in range(nz):
        lhs = left[:, z * rows : (z + 1) * rows]
        for out, core in ((keep, info[1]), (give, 1 - info[1])):
            out[z] = dot_tn(lhs, right[:, pl.ds(pl.multiple_of(core * cols, 128), cols)]).astype(BF)


def dense_place_kernel(nx, info, mine, recv, *outs):
    nz, per = outs[0].shape[:2]
    for kx in range(nx):
        x = lax.rem(info[3] + kx, nx)
        at = pl.ds(aligned(x * per, per), per)
        outs[kx][pl.ds(info[1] * (nz // 2), nz // 2)] = mine[:, at, :]
        outs[kx][pl.ds((1 - info[1]) * (nz // 2), nz // 2)] = recv[:, at, :]


def total_kernel(*refs):
    out = refs[-1]
    at = 0
    for ref in refs[:-1]:
        cols = ref.shape[2]
        total = ref[0].astype(F32)
        for z in range(1, ref.shape[0]):
            total = total + ref[z].astype(F32)
        out[:, at : at + cols] = total.astype(BF)
        at += cols


def fold_x_kernel(nx, *refs):
    out = refs[-1]
    cols = refs[0].shape[2]
    for p in range(len(refs) // nx):
        total = refs[p * nx][...].astype(F32)
        for kx in range(1, nx):
            total = total + refs[p * nx + kx][...].astype(F32)
        out[:, :, p * cols : (p + 1) * cols] = total.astype(BF)


def attention_back_kernel(n, rd, *refs):
    info, part, recv, residual, own, other, gain, qkv, probs, *rest = refs
    held, outs = rest[:n], rest[n:]
    other_half, res_ref, resb_ref, sums_ref, dqkv_ref, qvb_ref, wd, gctx, sem = outs
    load = Load(sem)
    load.dense(info, held, other_half, rd, wd)
    load.start()
    rows, width = own.shape
    half = width // 2
    hd = width // H
    for i, ref in enumerate((own, other)):
        here, there = slice(i * rows, (i + 1) * rows), slice((1 - i) * rows, (2 - i) * rows)
        grad_mid = part[here, :] + recv[there, :]
        normed, inv_std = layer_norm(residual[here, :])
        grad_res = ref[...].astype(F32) + norm_back(grad_mid * gain[...], normed, inv_std)
        resb_ref[here, :] = grad_res.astype(BF)
        if i == 0:
            res_ref[...] = grad_res
            sums_ref[0:1, :] = jnp.sum(grad_mid * normed, axis=0, keepdims=True)
            sums_ref[1:2, :] = jnp.sum(grad_mid, axis=0, keepdims=True)
            sums_ref[2:3, :] = jnp.sum(grad_res, axis=0, keepdims=True)
    load.wait()
    gctx[...] = dot_nt(resb_ref[...], wd[...]).astype(BF)

    lane = lax.broadcasted_iota(jnp.int32, (rows, 2 * hd), 1)
    first = lane < hd
    pairs = half // (2 * hd)
    qvb_ref[...] = jnp.zeros_like(qvb_ref)

    @pl.loop(0, 2 * pairs, unroll=8)
    def _(step):
        seq, pair = step // pairs, step % pairs
        at = pl.ds(pl.multiple_of(seq * rows, rows), rows)
        lanes = [pl.ds(pl.multiple_of(p * half + pair * 2 * hd, 2 * hd), 2 * hd) for p in range(3)]
        q, k, v = (qkv[at, where] for where in lanes)
        g = gctx[at, lanes[0]]
        dq, dk, dv = 0.0, 0.0, 0.0
        for i in range(2):
            mine = first if i == 0 else jnp.logical_not(first)
            g_i = jnp.where(mine, g, jnp.zeros_like(g))
            prob = probs[step * 2 + i]
            prob_f = prob.astype(F32)
            grad_probs = dot_nt(g_i, v)
            delta = jnp.sum(prob_f * grad_probs, axis=-1, keepdims=True)
            grad_scores = (prob_f * (grad_probs - delta) * hd ** (-0.5)).astype(BF)
            dq = dq + dot(grad_scores, jnp.where(mine, k, jnp.zeros_like(k)))
            dk = dk + dot_tn(grad_scores, jnp.where(mine, q, jnp.zeros_like(q)))
            dv = dv + dot_tn(prob, g_i)
        for where, value in zip(lanes, (dq, dk, dv)):
            dqkv_ref[at, where] = value.astype(BF)
        for row, value in ((0, dq), (1, dv)):
            qvb_ref[row : row + 1, lanes[0]] = qvb_ref[row : row + 1, lanes[0]] + jnp.sum(value, axis=0, keepdims=True)


def normed_kernel(n, rd, *refs):
    info, dqkv, *rest = refs
    pieces, (own_ref, other_ref, wq, sem) = rest[:n], rest[n:]
    load = Load(sem)
    load.qkv(info, pieces, rd, wq)
    load.start()
    load.wait()
    rows, width = own_ref.shape
    tile = 256

    @pl.loop(0, width // tile, unroll=4)
    def _(t):
        at = pl.ds(pl.multiple_of(t * tile, tile), tile)
        both = dot_nt(dqkv[...], wq[at, :])
        own_ref[:, at] = both[:rows]
        other_ref[:, at] = both[rows:]


def input_kernel(own, recv, hidden, grad_res, gain, in_ref, sums_ref):
    grad_normed = own[...] + recv[...]
    normed, inv_std = layer_norm(hidden[...].astype(F32))
    sums_ref[0:1, :] = jnp.sum(grad_normed * normed, axis=0, keepdims=True)
    sums_ref[1:2, :] = jnp.sum(grad_normed, axis=0, keepdims=True)
    in_ref[...] = grad_res[...] + norm_back(grad_normed * gain[...], normed, inv_std)


def pick(pair_first, pair_second, index):
    flip = index == 1
    return jnp.where(flip, pair_second, pair_first), jnp.where(flip, pair_first, pair_second)


def on_device(
    reps,
    shards,
    hidden_in,
    cotangent,
    ln1_gain,
    ln1_bias,
    w_qkv,
    qv_bias,
    w_dense,
    dense_bias,
    ln2_gain,
    ln2_bias,
    w_up,
    up_bias,
    w_down,
    down_bias,
):
    at = Place(reps, shards)
    info, core, y = at.info, at.core, at.y
    nz, nx, n = at.nz, at.nx, shards
    rows, width = hidden_in.shape
    rd = w_qkv.shape[0]
    ff = w_up.shape[1]
    quarter = ff // shards // 4
    half = width // 2
    heads = H // 2
    hd = width // H
    fq = shards * quarter
    dma = pltpu.SemaphoreType.DMA
    slopes = jnp.asarray(2.0 ** (-8.0 * (np.arange(H) + 1.0) / H), F32)
    slopes = lax.dynamic_slice_in_dim(slopes, core * heads, heads)

    qkv_half = lax.dynamic_index_in_dim(w_qkv.reshape(rd, 3, 2, half), core, 2, keepdims=False)
    qkv_half = qkv_half.reshape(rd, 3 * half)
    cut = 3 * half // 2
    qkv_first = at.gather(qkv_half[:, :cut])
    hidden_other = at.to_core(hidden_in)

    vectors = (ln1_gain, ln1_bias, qv_bias, dense_bias, ln2_gain, ln2_bias, up_bias, down_bias)
    packed = jnp.concatenate(vectors)
    size = packed.shape[0]
    packed = jnp.pad(packed, (0, 16 * cut - size)).reshape(16, cut)
    qkv_second = at.gather(jnp.concatenate([qkv_half[:, cut:], packed]))
    qkv_pieces = qkv_first + qkv_second
    lines = -(-size // cut)
    held = jnp.stack([v[:, rd : rd + lines].reshape(nz, -1)[:, :size] for v in qkv_second])
    held = jnp.stack([lax.dynamic_index_in_dim(held, (at.x - x) % nx, 0, keepdims=False) for x in range(nx)], axis=1)
    packed = held.reshape(n, size).astype(F32)
    whole, start = [], 0
    for v in vectors:
        whole.append(packed[:, start : start + v.shape[0]].reshape(1, -1))
        start += v.shape[0]
    gain1, bias1, qv_b, dense_b, gain2, bias2, up_b, down_b = whole
    qv_half = lax.dynamic_index_in_dim(qv_b.reshape(2, 2, half), core, 1, keepdims=False)
    qkv_bias = jnp.concatenate([qv_half[:1], jnp.zeros((1, half), F32), qv_half[1:]], axis=1)
    up_b4 = lax.dynamic_index_in_dim(up_b.reshape(n, 2, 2, quarter), core, 1, keepdims=False)
    up_halves = jnp.concatenate(pick(up_b4[:, 0].reshape(1, -1), up_b4[:, 1].reshape(1, -1), y), axis=1)

    up_quarter = w_up.reshape(rd, n, 4, quarter)
    up_quarter = lax.dynamic_index_in_dim(up_quarter, core * 2 + y, 2, keepdims=False).reshape(rd, fq)
    up_first = at.gather(up_quarter[:, : fq // 2], True)
    dense_held = at.gather(lax.dynamic_slice_in_dim(w_dense, core * half, half, 1))
    give = jnp.stack([lax.dynamic_slice_in_dim(v, (1 - core) * (nz // 2), nz // 2, 0) for v in dense_held])
    dense_in = dense_held + [at.to_core(give)]
    up_second = at.gather(up_quarter[:, fq // 2 :], True)
    split = width * 5 // 8
    down_half = lax.dynamic_slice_in_dim(w_down, core * 2 * quarter, 2 * quarter, 0)
    down_quarter = lax.dynamic_slice_in_dim(down_half, y * quarter, quarter, 0)
    down_pieces = at.gather(down_quarter[:, :split], True)
    up_pieces = [v for i in range(2) for p in (up_first, up_second) for v in p[i * nx : (i + 1) * nx]]
    down_pieces = down_pieces + at.gather(down_half[:, split:])
    cot_other = at.to_core(cotangent)

    mac = 2 * 2 * rows * width
    nin, qkv, ctx, probs = call(
        functools.partial(attention_kernel, 2 * nx, rd),
        [((2 * rows, width), BF), ((2 * rows, 3 * half), BF), ((2 * rows, half), BF), ((2 * heads, rows, rows), BF)],
        [info, slopes, after(hidden_in, up_first[:1]), hidden_other, gain1, bias1, qkv_bias] + qkv_pieces,
        "ss" + "v" * 5 + "a" * 2 * nx,
        [pltpu.VMEM((width, 3 * half), BF), dma((2 * n,))],
        mac * 4 * half,
        "attn",
    )
    (part,) = call(
        functools.partial(dense_kernel, nx, rd),
        [((2 * rows, width), F32)],
        [info, after(ctx, up_second[:1])] + dense_in,
        "sv" + "a" * (nx + 1),
        [pltpu.VMEM((half, width), BF), dma((n,))],
        mac * half,
        "dense",
    )
    residual, mid = call(
        middle_kernel,
        [((2 * rows, width), F32), ((2 * rows, width), BF)],
        [after(hidden_in, up_second[1:nx] + down_pieces[:1]), hidden_other, part, at.to_core(part), dense_b, gain2, bias2],
        "v" * 7,
        name="middle",
    )
    act, slope = call(
        functools.partial(up_kernel, 4 * nx, rd),
        [((2 * rows, 2 * fq), BF), ((2 * rows, 2 * fq), F32)],
        [info, mid, up_halves] + up_pieces,
        "svv" + "a" * 4 * nx,
        [pltpu.VMEM((width, 2 * fq), BF), dma((4 * n,))],
        mac * 2 * fq,
        "up",
    )

    def scatter_y(left, right, per, cols, by_y, name):
        cols //= 2
        terms = call(
            functools.partial(grad_y_kernel, 2, by_y),
            [((nz, nx * per, cols), BF)] * 4,
            [info, left] + right,
            "sv" + "v" * len(right),
            name=name,
        )
        return [(terms[2 * p + 1], at.to_y(terms[2 * p])) for p in range(2)]

    def fold_y(terms, name):
        nz_, rows_, cols = terms[0].shape
        out = call(
            functools.partial(fold_y_kernel, nx),
            [((nz, rows_ // nx, cols), BF)] * nx,
            [info] + list(terms),
            "svv",
            name=name + "_y",
        )
        return over_x(out)

    def over_x(parts):
        return [parts[0]] + [at.to_x(parts[kx], kx) for kx in range(1, nx)]

    def fold_x(ins, name):
        nz_, per, cols = ins[0].shape
        outs = [((nz, per, cols * len(ins) // nx), BF)]
        return call(functools.partial(fold_x_kernel, nx), outs, ins, "v" * len(ins), name=name + "_x")[0]

    def finish_z(ends, name):
        _, per, cols = ends[0].shape
        total = sum(v.shape[2] for v in ends)
        return call(total_kernel, [((per, total), BF)], ends, "v" * len(ends), name=name + "_z")[0]

    down_x, before = [], []
    for p in range(2):
        down_terms = call(
            functools.partial(down_grad_kernel, p, nx),
            [((nz, 2 * quarter, width // 2), BF)] * nx,
            [info, after(act, before), cotangent, cot_other],
            "svvv",
            name="gdown",
        )
        before = [down_terms[0]]
        down_x.append(over_x(down_terms))

    gpre, gpre_sums, gmid = call(
        functools.partial(feed_back_kernel, 4 * nx, rd, quarter),
        [((2 * rows, 2 * fq), BF), ((1, 2 * fq), F32), ((2 * rows, width), F32)],
        [info, cotangent, cot_other, slope] + up_pieces + down_pieces,
        "svvv" + "a" * 7 * nx,
        [pltpu.VMEM((width, 2 * fq), BF), pltpu.VMEM((2 * fq, width), BF), dma((4 * n,)), dma((4 * n,))],
        mac * 4 * fq,
        "feed_back",
    )
    gmid_recv = at.to_core(gmid)
    up_terms = call(
        functools.partial(up_grad_kernel, 2, nx),
        [((nz, nx * rd, fq // 2), BF)] * 4,
        [mid, gpre],
        "vv",
        name="gup",
    )
    up_y = [(up_terms[2 * p + 1], at.to_y(up_terms[2 * p])) for p in range(2)]
    down_sum = fold_x(after(down_x[0], [up_terms[0]]), "gdown")
    end_down = [at.swap_z(down_sum)]

    grad_res, grad_res_b, sums2, dqkv, qv_sums = call(
        functools.partial(attention_back_kernel, nx, rd),
        [
            ((rows, width), F32),
            ((2 * rows, width), BF),
            ((3, width), F32),
            ((2 * rows, 3 * half), BF),
            ((2, half), F32),
        ],
        [info, after(gmid, [down_sum]), gmid_recv, residual, cotangent, cot_other, gain2, qkv, probs] + dense_in,
        "s" + "v" * 8 + "a" * (nx + 1),
        [pltpu.VMEM((half, width), BF), pltpu.VMEM((2 * rows, half), BF), dma((n,))],
        mac * 3 * half,
        "attn_back",
    )
    qkv_terms = scatter_y(nin, [dqkv], rd, cut, True, "gqkv")
    last = [qkv_terms[0][0]]

    def order(value):
        last[:] = [value[0] if isinstance(value, (list, tuple)) else value]
        return value

    down_sum2 = order(fold_x(after(down_x[1], last), "gdown"))
    end_down.append(at.swap_z(after(down_sum2, end_down)))
    up_x = order(fold_y(after(up_y[0], last), "gup"))
    keep, give = call(
        dense_grad_kernel,
        [((nz // 2, nx * rd, half), BF)] * 2,
        [info, after(ctx, last), grad_res_b],
        "svv",
        name="gdense",
    )
    order(keep)
    out_own, out_other = order(
        call(
            functools.partial(output_kernel, 3 * nx, quarter),
            [((rows, width), F32), ((rows, width), F32)],
            [info, after(act, last)] + down_pieces,
            "sv" + "a" * 3 * nx,
            [pltpu.VMEM((2 * fq, width), BF), dma((4 * n,))],
            name="output",
        )
    )
    up_x = up_x + order(fold_y(after(up_y[1], last), "gup"))
    parts = call(
        functools.partial(dense_place_kernel, nx),
        [((nz, rd, half), BF)] * nx,
        [info, after(keep, last), at.to_core(give)],
        "svv",
        name="gdense_c",
    )
    order(parts)
    dense_x = over_x(parts)
    up_sum = order(fold_x(after(up_x, last), "gup"))
    end_up = at.swap_z(after(up_sum, end_down[1:]))
    order(end_down[1])
    qkv_x = order(fold_y(after(qkv_terms[0], last), "gqkv"))
    qkv_x = qkv_x + order(fold_y(after(qkv_terms[1], last), "gqkv"))
    order(end_up)
    norm_own, norm_other = order(
        call(
            functools.partial(normed_kernel, 2 * nx, rd),
            [((rows, width), F32), ((rows, width), F32)],
            [info, after(dqkv, last)] + qkv_pieces,
            "sv" + "a" * 2 * nx,
            [pltpu.VMEM((width, 3 * half), BF), dma((2 * n,))],
            name="gnorm",
        )
    )
    qkv_sum = order(fold_x(after(qkv_x, last), "gqkv"))
    end_qkv = at.swap_z(after(qkv_sum, [end_up]))
    order(end_up)
    down_part = order(finish_z(after(end_down, last), "gdown"))
    down_recv = at.to_y(down_part)
    dense_sum = order(fold_x(after(dense_x, last), "gdense"))
    end_dense = at.swap_z(after(dense_sum, [end_qkv]))
    up_own = order(finish_z([after(end_up, last)], "gup"))
    up_other = at.to_y(up_own)
    order(end_qkv)
    qkv_own = order(finish_z([after(end_qkv, last)], "gqkv"))
    qkv_other = at.to_y(qkv_own)
    dense_part = order(finish_z([after(end_dense, last)], "gdense"))
    dense_mine = dense_part.astype(F32) + at.to_y(dense_part).astype(F32)
    grad_dense = jnp.concatenate(pick(dense_mine, at.to_core(dense_mine), core), axis=1)

    output = (residual[:rows] + (after(out_own, [dense_part]) + at.to_core(out_other)) + down_b).astype(BF)

    input_grad, sums1 = call(
        input_kernel,
        [((rows, width), F32), ((2, width), F32)],
        [norm_own, at.to_core(norm_other), hidden_in, grad_res, gain1],
        "v" * 5,
        name="input_grad",
    )

    down_c = down_part.astype(F32) + down_recv.astype(F32)
    grad_down = jnp.concatenate(pick(down_c, at.to_core(down_c), core), axis=0)
    up_c = jnp.stack([v.reshape(rd, n, quarter) for v in pick(up_own, up_other, y)], axis=2)
    grad_up = jnp.stack(pick(up_c, at.to_core(up_c), core), axis=2).reshape(rd, ff).astype(F32)
    qkv_c = jnp.concatenate(pick(qkv_own, qkv_other, y), axis=1).reshape(rd, 3, 1, half)
    grad_qkv = jnp.concatenate(pick(qkv_c, at.to_core(qkv_c), core), axis=2).reshape(rd, 3 * width).astype(F32)

    grad_down_bias = jnp.sum(cotangent.astype(F32), axis=0)
    up_y = jnp.stack([g.reshape(n, quarter) for g in pick(gpre_sums[0, :fq], gpre_sums[0, fq:], y)], axis=1)
    on_core = jnp.arange(2) == core
    up_bias_all = jnp.where(on_core[None, :, None, None], up_y[:, None], 0.0).reshape(-1)
    qv_all = jnp.where(on_core[None, :, None], qv_sums[:, None], 0.0).reshape(-1)
    feed = jnp.concatenate([sums2.reshape(-1), grad_down_bias, up_bias_all, sums1.reshape(-1), qv_all])
    feed = at.sum_all(feed[None, :])[0]

    def own(start, size):
        per = size // n
        return lax.dynamic_slice_in_dim(feed, start + at.shard * per, per)

    return (
        output,
        input_grad,
        own(4 * width + ff, width),
        own(5 * width + ff, width),
        grad_qkv,
        own(6 * width + ff, 2 * width),
        grad_dense,
        own(2 * width, width),
        own(0, width),
        own(width, width),
        grad_up,
        own(4 * width, ff),
        grad_down,
        own(3 * width, width),
    )


def solution(mesh):
    both, rows, vector = P(("rep", "shard"), None), P("shard", None), P("shard")
    weights = (vector, vector, rows, vector, rows, vector, vector, vector, rows, vector, rows, vector)
    return jax.shard_map(
        functools.partial(on_device, mesh.shape["rep"], mesh.shape["shard"]),
        mesh=mesh,
        in_specs=(both, both) + weights,
        out_specs=(both, both) + weights,
        check_vma=False,
    )
```
